256 devices in a mesh: ctx: 64 (over x, y_hi, z), resp: 4 (over y_lo, core).
Axes of the slice: x: 4, y: 4 (y_hi: 2, y_lo: 2; y = y_hi * 2 + y_lo), z: 8, core: 2. Of those that a mesh axis runs over, the one named last changes fastest.
Arguments:
- queries: bfloat16 [4, 8192, 2560], P('resp', 'ctx'), may hold values from -30 to 30
- cotangent: bfloat16 [4, 8192, 2560], P('resp', 'ctx'), may hold values from -24 to 24
- sampled_keys: bfloat16 [4, 8192, 512], P('resp', 'ctx'), may hold values from -6 to 6
- sampled_values: bfloat16 [4, 8192, 512], P('resp', 'ctx'), may hold values from -6 to 6
- shared_prompt_keys: bfloat16 [512, 512], P('ctx'), may hold values from -6 to 6
- shared_prompt_values: bfloat16 [512, 512], P('ctx'), may hold values from -6 to 6
- lengths: int32 [4, 8], P('resp'), may hold values from 1 to 2048, 8192 in all within a row
Outputs:
- query_gradient: bfloat16 [4, 8192, 2560], P('resp', 'ctx')
- shared_key_gradient: bfloat16 [512, 512], P('ctx')
- shared_value_gradient: bfloat16 [512, 512], P('ctx')
The draws below stay inside these ranges and needn't reach their ends.
Inputs may be any that keep to these rules, and one draw needn't show every extreme that they name: Each row holds the lengths of the 8 responses packed one after another into the group's 8192 positions; a row sums to 8192, and its longest response has exactly 2048 positions.
All inputs are finite; a program needn't handle non-finite values.
Results may differ from the reference program's by a relative error of at most 0.0053.
Values may be sent and summed in bfloat16 or wider, within the bound.
A program may use at most 128 MiB of HBM per device.

```python
import math
import jax
import jax.numpy as jnp
import numpy as np
from jax import lax

HEAD_WIDTH = 128
KEY_VALUE_HEADS = 4
QUERY_PER_KEY = 5
RESPONSE_LOCAL = 128
HQ = 20
LONGEST_LENGTH = 2048
RESPONSE_GROUPS = 4
GROUP_TOKENS = 8192
PROMPT_LENGTH = 512
NSEG = 8


def draw_queries(key, part):
    key = jax.random.fold_in(key, 17)
    return jnp.clip(jax.random.normal(key, (RESPONSE_GROUPS, GROUP_TOKENS, KEY_VALUE_HEADS * QUERY_PER_KEY * HEAD_WIDTH), jnp.float32), -6.0, 6.0).astype(jnp.bfloat16)


def draw_shared_prompt_keys(key, part):
    key = jax.random.fold_in(key, 29)
    return jnp.clip(jax.random.normal(key, (PROMPT_LENGTH, KEY_VALUE_HEADS * HEAD_WIDTH), jnp.float32), -6.0, 6.0).astype(jnp.bfloat16)


def steps_of(rng, extent, shards, low, top_value):
    def one(position, shards_of):
        steps = jax.random.uniform(jax.random.fold_in(jax.random.fold_in(rng, 6), position), (shards_of,), jnp.float32, low / len(shards), top_value / len(shards))
        return jnp.repeat(jnp.exp(steps), extent[position] // shards_of).reshape((-1,) + (1,) * (len(extent) - position - 1))

    loudness = one(*shards[0])
    for cut in shards[1:]:
        loudness = loudness * one(*cut)
    return loudness


def length_profile(count, total, limit, lean):
    loads = [(1 << 20) // math.isqrt(standing ** lean) + 1 for standing in range(2, count + 1)]
    spare, holding = total - limit - (count - 1), [1] * (count - 1)
    while spare > 0:
        free = [i for i in range(count - 1) if holding[i] < limit]
        whole, budget = sum([loads[i] for i in free]), spare
        for i in free:
            extra = min(limit - holding[i], max(1, budget * loads[i] // whole), spare)
            holding[i] = holding[i] + extra
            spare = spare - extra
    return np.array([limit] + holding)


def ragged_sizes(stream_key, number_of, total, reach, skew):
    if number_of == 2:
        one = jax.random.randint(stream_key, (), max(1, total - reach), min(reach, total - 1) + 1)
        return jnp.stack([one, total - one])
    tallies = jnp.asarray(length_profile(number_of, total, reach, skew), jnp.int32)
    pairs = (number_of - 1) // 2
    donor, receiver = tallies[1:1 + 2 * pairs:2], tallies[2:2 + 2 * pairs:2]
    slack = jnp.minimum(donor - 1, reach - receiver)
    passed = jax.random.randint(jax.random.fold_in(stream_key, 1), (pairs,), 0, 1 << 20) % (slack + 1)
    tallies = tallies.at[1:1 + 2 * pairs:2].set(donor - passed).at[2:2 + 2 * pairs:2].set(receiver + passed)
    return tallies[jax.random.permutation(jax.random.fold_in(stream_key, 2), number_of)]


def scatter_about(rng, shape, spread, limit, cuts=(), held_as=jnp.bfloat16):
    result = spread * jax.random.normal(rng, shape, jnp.float32)
    if cuts:
        result = result * steps_of(rng, shape, cuts, -0.22, 0.18)
    return jnp.clip(result, -limit, limit).astype(held_as)


def setup_inputs(seed: int = 0) -> dict:
    key_of = jax.random.split(jax.random.key(seed), 8)
    return {
        "queries": draw_queries(jax.random.fold_in(key_of[7], 71), 0),
        "cotangent": scatter_about(key_of[1], (RESPONSE_GROUPS, GROUP_TOKENS, HQ * HEAD_WIDTH), 4.0, 24.0, ((0, 4), (1, 64))),
        "sampled_keys": scatter_about(key_of[2], (RESPONSE_GROUPS, GROUP_TOKENS, KEY_VALUE_HEADS * HEAD_WIDTH), 1.0, 6.0, ((0, 4), (1, 64))),
        "sampled_values": scatter_about(key_of[3], (RESPONSE_GROUPS, GROUP_TOKENS, KEY_VALUE_HEADS * HEAD_WIDTH), 1.0, 6.0, ((0, 4), (1, 64))),
        "shared_prompt_keys": draw_shared_prompt_keys(jax.random.fold_in(key_of[7], 71), 0),
        "shared_prompt_values": scatter_about(key_of[5], (PROMPT_LENGTH, KEY_VALUE_HEADS * HEAD_WIDTH), 1.0, 6.0, ((0, 64),)),
        "lengths": jax.vmap(lambda own: ragged_sizes(own, NSEG, GROUP_TOKENS, LONGEST_LENGTH, 2))(jax.random.split(key_of[6], RESPONSE_GROUPS)).reshape((RESPONSE_GROUPS, NSEG)).astype(jnp.int32),
    }


def segment_of(length_row, positions):
    segment_ends = jnp.cumsum(length_row)
    return jnp.sum((segment_ends[None, :] <= positions[:, None]).astype(jnp.int32), axis=1)


def reference(queries, cotangent, sampled_keys, sampled_values, shared_prompt_keys, shared_prompt_values, lengths):
    score_scale = HEAD_WIDTH ** -0.5
    blocks = GROUP_TOKENS // RESPONSE_LOCAL
    shared_key_heads = shared_prompt_keys.astype(jnp.float32).reshape(PROMPT_LENGTH, KEY_VALUE_HEADS, HEAD_WIDTH)
    shared_value_heads = shared_prompt_values.astype(jnp.float32).reshape(PROMPT_LENGTH, KEY_VALUE_HEADS, HEAD_WIDTH)
    padding_rows = jnp.zeros((RESPONSE_GROUPS, LONGEST_LENGTH, KEY_VALUE_HEADS * HEAD_WIDTH), sampled_keys.dtype)
    widened_keys = jnp.concatenate([padding_rows, sampled_keys], axis=1)
    widened_values = jnp.concatenate([padding_rows, sampled_values], axis=1)

    def block_step(running, block_index):
        key_gradient_sum, value_gradient_sum = running
        current_group_index = (block_index // blocks).astype(jnp.int32)
        start_offset = ((block_index % blocks) * RESPONSE_LOCAL).astype(jnp.int32)
        zero_value = jnp.zeros((), jnp.int32)
        block_of_queries = lax.dynamic_slice(queries, (current_group_index, start_offset, zero_value), (1, RESPONSE_LOCAL, HQ * HEAD_WIDTH))[0]
        block_of_queries = block_of_queries.astype(jnp.float32).reshape(RESPONSE_LOCAL, KEY_VALUE_HEADS, QUERY_PER_KEY, HEAD_WIDTH)
        block_cotangent = lax.dynamic_slice(cotangent, (current_group_index, start_offset, zero_value), (1, RESPONSE_LOCAL, HQ * HEAD_WIDTH))[0]
        block_cotangent = block_cotangent.astype(jnp.float32).reshape(RESPONSE_LOCAL, KEY_VALUE_HEADS, QUERY_PER_KEY, HEAD_WIDTH)
        keys_in_window = lax.dynamic_slice(widened_keys, (current_group_index, start_offset, zero_value), (1, LONGEST_LENGTH + RESPONSE_LOCAL, KEY_VALUE_HEADS * HEAD_WIDTH))[0]
        values_in_window = lax.dynamic_slice(widened_values, (current_group_index, start_offset, zero_value), (1, LONGEST_LENGTH + RESPONSE_LOCAL, KEY_VALUE_HEADS * HEAD_WIDTH))[0]
        keys_in_window = keys_in_window.astype(jnp.float32).reshape(LONGEST_LENGTH + RESPONSE_LOCAL, KEY_VALUE_HEADS, HEAD_WIDTH)
        values_in_window = values_in_window.astype(jnp.float32).reshape(LONGEST_LENGTH + RESPONSE_LOCAL, KEY_VALUE_HEADS, HEAD_WIDTH)
        length_row = lax.dynamic_slice(lengths, (current_group_index, zero_value), (1, NSEG))[0]
        query_pos = start_offset + jnp.arange(RESPONSE_LOCAL, dtype=jnp.int32)
        key_pos = start_offset - LONGEST_LENGTH + jnp.arange(LONGEST_LENGTH + RESPONSE_LOCAL, dtype=jnp.int32)
        query_segment = segment_of(length_row, query_pos)
        key_segment = segment_of(length_row, key_pos)
        visible = (key_pos[None, :] >= 0) & (key_pos[None, :] <= query_pos[:, None]) & (key_segment[None, :] == query_segment[:, None])
        visible = jnp.concatenate([jnp.ones((RESPONSE_LOCAL, PROMPT_LENGTH), bool), visible], axis=1)
        all_keys = jnp.concatenate([shared_key_heads, keys_in_window], axis=0)
        all_values = jnp.concatenate([shared_value_heads, values_in_window], axis=0)
        logits = jnp.einsum('rkqd,jkd->rkqj', block_of_queries, all_keys) * score_scale
        logits = jnp.where(visible[:, None, None, :], logits, -jnp.inf)
        top_score = jnp.max(logits, axis=-1)
        weights = jnp.exp(logits - top_score[..., None])
        total = jnp.sum(weights, axis=-1)
        probs = weights / total[..., None]
        prob_grad = jnp.einsum('rkqd,jkd->rkqj', block_cotangent, all_values)
        row_delta = jnp.sum(probs * prob_grad, axis=-1)
        logit_grad = score_scale * probs * (prob_grad - row_delta[..., None])
        logit_low = lax.optimization_barrier(logit_grad.astype(jnp.bfloat16)).astype(jnp.float32)
        probs_low = lax.optimization_barrier(probs.astype(jnp.bfloat16)).astype(jnp.float32)
        query_grad = jnp.einsum('rkqj,jkd->rkqd', logit_low, all_keys)
        query_grad = query_grad.astype(jnp.bfloat16).reshape(RESPONSE_LOCAL, HQ * HEAD_WIDTH)
        key_terms = jnp.einsum('rkqj,rkqd->jkd', logit_low[..., :PROMPT_LENGTH], block_of_queries)
        value_terms = jnp.einsum('rkqj,rkqd->jkd', probs_low[..., :PROMPT_LENGTH], block_cotangent)
        return (key_gradient_sum + key_terms, value_gradient_sum + value_terms), query_grad

    initial_carry = (jnp.zeros((PROMPT_LENGTH, KEY_VALUE_HEADS, HEAD_WIDTH), jnp.float32), jnp.zeros((PROMPT_LENGTH, KEY_VALUE_HEADS, HEAD_WIDTH), jnp.float32))
    (key_gradient_sum, value_gradient_sum), query_blocks = lax.scan(block_step, initial_carry, jnp.arange(RESPONSE_GROUPS * blocks, dtype=jnp.int32))
    query_gradient = query_blocks.reshape(RESPONSE_GROUPS, GROUP_TOKENS, HQ * HEAD_WIDTH)
    shared_key_gradient = key_gradient_sum.reshape(PROMPT_LENGTH, KEY_VALUE_HEADS * HEAD_WIDTH).astype(jnp.bfloat16)
    shared_value_gradient = value_gradient_sum.reshape(PROMPT_LENGTH, KEY_VALUE_HEADS * HEAD_WIDTH).astype(jnp.bfloat16)
    return (query_gradient, shared_key_gradient, shared_value_gradient)
```

```python
import functools

import jax
import jax.numpy as jnp
from jax import lax
from jax.experimental import pallas as pl
from jax.experimental.pallas import tpu as pltpu
from jax.sharding import PartitionSpec as P

D = 128
KVH = 4
QPK = 5
HQ = KVH * QPK
T = 128
PR = 512
G = QPK * T
NZ = 8
NXY = 8
UP = 4
DOWN = NZ - 1 - UP
SCALE = D ** (-0.5)
LOG2E = 1.4426950408889634
NEG = -1e30
OWN = 16
PROMPT = 17 * T
KEYS = 17 * T + PR
MESH = pl.DeviceIdType.MESH


def remote(src, dst, send, recv, ctx, resp):
    return pltpu.make_async_remote_copy(
        src_ref=src,
        dst_ref=dst,
        send_sem=send,
        recv_sem=recv,
        device_id=(ctx, resp),
        device_id_type=MESH,
    )


def place():
    c = lax.axis_index("ctx")
    r = lax.axis_index("resp")
    z = lax.rem(c, NZ)
    xy = c // NZ
    role = lax.rem(r, 2)
    return c, r, z, xy, role, r + 1 - 2 * role


def greet(peers):
    barrier = pltpu.get_barrier_semaphore()
    for ctx, resp in peers:
        pl.semaphore_signal(barrier, inc=1, device_id=(ctx, resp), device_id_type=MESH)
    pl.semaphore_wait(barrier, len(peers))


class Gather:
    def __init__(self, kv, pg, za, ks, kr, ps, pr):
        self.kv, self.pg, self.za = kv, pg, za
        self.ks, self.kr, self.ps, self.pr = ks, kr, ps, pr
        self.c, self.r, self.z, self.xy, self.role, self.mate = place()

    def peers(self):
        out = []
        for s in range(1, NZ):
            out.append((self.xy * NZ + lax.rem(self.z + s, NZ), self.r))
        for s in range(1, NXY):
            out.append((lax.rem(self.xy + s, NXY) * NZ + self.z, self.r))
        out.append((self.c, self.mate))
        return out

    def piece(self, src, dst, send, ctx):
        return remote(self.kv.at[src], self.kv.at[dst], self.ks.at[send], self.kr.at[dst], ctx, self.r)

    def arrived(self, slot):
        self.piece(slot, slot, slot, self.c).wait_recv()

    def own_sends(self):
        z = self.z
        after = lax.rem(self.c + NZ, NZ * NXY)
        second = lax.rem(self.c + 2 * NZ, NZ * NXY)
        return [
            (None, self.piece(OWN, z, 17, second)),
            (None, self.piece(OWN, 8 + z, 16, after)),
            (z < NZ - 1, self.piece(OWN, z, 18, self.c + 1)),
        ]

    def step(self, s):
        z, c = self.z, self.c
        up = self.xy * NZ + lax.rem(z + 1, NZ)
        down = self.xy * NZ + lax.rem(z + NZ - 1, NZ)
        if s == 0:
            return [
                (None, z, [(z > 0, self.piece(z, z, z, down))]),
                (
                    None,
                    8 + z,
                    [(None, self.piece(8 + z, 8 + z, 19, up)), (None, self.piece(8 + z, 8 + z, 8 + z, down))],
                ),
            ]
        low, high = lax.rem(z - s + NZ, NZ), lax.rem(z + s, NZ)
        out = [
            (z >= s, low, [(z < NZ - 1, self.piece(low, low, low, up))]),
            (z + s < NZ, high, [(z > 0, self.piece(high, high, high, down))]),
        ]
        if s <= UP:
            out.append((None, 8 + low, [(None, self.piece(8 + low, 8 + low, 8 + low, up))] if s < UP else []))
        if s <= DOWN:
            out.append((None, 8 + high, [(None, self.piece(8 + high, 8 + high, 8 + high, down))] if s < DOWN else []))
        return out

    @staticmethod
    def when(condition, do):
        if condition is None:
            do()
        else:
            pl.when(condition)(do)

    def start_own(self):
        for condition, copy in self.own_sends():
            self.when(condition, copy.start)

    def take_step(self, s):
        for condition, slot, sends in self.step(s):

            def take(slot=slot, sends=sends):
                self.arrived(slot)
                for inner, copy in sends:
                    self.when(inner, copy.start)

            self.when(condition, take)

    def finish(self):
        for condition, copy in self.own_sends():
            self.when(condition, copy.wait_send)
        for s in range(NZ):
            for condition, slot, sends in self.step(s):

                def done(sends=sends):
                    for inner, copy in sends:
                        self.when(inner, copy.wait_send)

                self.when(condition, done)

    def prompt_z(self, pk, pv):
        z = self.z
        mine = jnp.where(self.role == 0, pk[...].astype(jnp.float32), pv[...].astype(jnp.float32))
        self.za[z] = mine
        self.zcopies = [
            remote(
                self.za.at[z],
                self.za.at[z],
                self.ps.at[s],
                self.pr.at[s],
                self.xy * NZ + lax.rem(z + s, NZ),
                self.r,
            )
            for s in range(1, NZ)
        ]
        for copy in self.zcopies:
            copy.start()

    def prompt_xy(self):
        for s, copy in enumerate(self.zcopies, 1):
            source = lax.rem(self.z - s + NZ, NZ)
            remote(self.za.at[source], self.za.at[source], self.ps.at[s], self.pr.at[s], self.c, self.r).wait_recv()
        rows = pl.ds(pl.multiple_of(self.xy * 64, 64), 64)
        self.pg[self.role, rows, :] = self.za[...].reshape(64, 512).astype(jnp.bfloat16)
        self.xycopies = [
            remote(
                self.pg.at[self.role, rows],
                self.pg.at[self.role, rows],
                self.ps.at[8 + s],
                self.pr.at[8 + s],
                lax.rem(self.xy + s, NXY) * NZ + self.z,
                self.r,
            )
            for s in range(1, NXY)
        ]
        for copy in self.xycopies:
            copy.start()

    def prompt_core(self):
        for s in range(1, NXY):
            source = lax.rem(self.xy - s + NXY, NXY)
            rows = pl.ds(pl.multiple_of(source * 64, 64), 64)
            block = self.pg.at[self.role, rows]
            remote(block, block, self.ps.at[8 + s], self.pr.at[8 + s], self.c, self.r).wait_recv()
        half = self.pg.at[self.role]
        self.corecopy = remote(half, half, self.ps.at[0], self.pr.at[0], self.c, self.mate)
        self.corecopy.start()

    def prompt_done(self):
        other = self.pg.at[1 - self.role]
        remote(other, other, self.ps.at[0], self.pr.at[0], self.c, self.mate).wait_recv()
        for copy in self.zcopies + self.xycopies + [self.corecopy]:
            copy.wait_send()


def gather_kernel(k, v, pk, pv, kv, pg, za, ks, kr, ps, pr):
    g = Gather(kv, pg, za, ks, kr, ps, pr)
    kv[OWN, :, :512] = k[...]
    kv[OWN, :, 512:] = v[...]
    greet(g.peers())
    g.prompt_z(pk, pv)
    g.start_own()
    g.prompt_xy()
    g.take_step(0)
    g.prompt_core()
    for s in range(1, NZ):
        g.take_step(s)
    g.prompt_done()
    g.finish()


class Attend:
    def __init__(self, q, do, kv, pg, lengths, sc):
        self.q, self.do, self.kv, self.pg, self.lengths = q, do, kv, pg, lengths
        (self.qt, self.dot_, self.qn, self.don, self.e, self.dp, self.m, self.l, self.w, self.mb, self.dq) = sc

    def prepare(self):
        for k in range(KVH):
            for h in range(QPK):
                cols = slice((k * QPK + h) * D, (k * QPK + h + 1) * D)
                rows = slice(h * T, (h + 1) * T)
                self.qn[k, rows, :] = self.q[:, cols]
                self.don[k, rows, :] = self.do[:, cols]
                self.qt[k, :, rows] = self.q[:, cols].T
                self.dot_[k, :, rows] = self.do[:, cols].T
        self.m[...] = jnp.full(self.m.shape, NEG, jnp.float32)
        self.l[...] = jnp.zeros(self.l.shape, jnp.float32)
        self.w[...] = jnp.zeros(self.w.shape, jnp.float32)
        self.dq[...] = jnp.zeros(self.dq.shape, jnp.float32)
        c = lax.axis_index("ctx")
        self.first = c * T
        self.qpos = self.first + lax.broadcasted_iota(jnp.int32, (1, T), 1)
        start = jnp.zeros((1, T), jnp.int32)
        end = jnp.int32(0)
        for s in range(8):
            end = end + self.lengths[0, s]
            start = jnp.where(self.qpos >= end, end, start)
        self.start = start

    def bias(self, slot):
        c = lax.axis_index("ctx")
        z = lax.rem(c, NZ)
        if isinstance(slot, int) and slot == OWN:
            base = c
        else:
            part = lax.rem(slot, NZ)
            near = c - z + part
            base = jnp.where(slot < NZ, jnp.where(part < z, near, near - 2 * NZ), near - NZ)
        pos = base * T + lax.broadcasted_iota(jnp.int32, (T, T), 0)
        visible = (pos >= self.start) & (pos <= self.qpos)
        return jnp.where(visible, 0.0, NEG).astype(jnp.float32)

    def forward(self, keys, values, bias, row, block, n):
        @pl.loop(0, KVH)
        def _(k):
            s = jnp.dot(keys(k), self.qt[k], preferred_element_type=jnp.float32)
            dp = jnp.dot(values(k), self.dot_[k], preferred_element_type=jnp.float32)
            self.dp[k, pl.ds(row, n), :] = dp
            for h in range(QPK):
                cols = slice(h * T, (h + 1) * T)
                x = s[:, cols] * (SCALE * LOG2E)
                if bias is not None:
                    x = x + bias
                old = self.m[k, :, cols]
                new = jnp.maximum(old, jnp.max(x, axis=0, keepdims=True))
                f = jnp.exp2(old - new)
                e = jnp.exp2(x - new)
                self.m[k, :, cols] = new
                self.mb[block, k, :, cols] = new
                self.l[k, :, cols] = self.l[k, :, cols] * f + jnp.sum(e, axis=0, keepdims=True)
                self.w[k, :, cols] = self.w[k, :, cols] * f + jnp.sum(e * dp[:, cols], axis=0, keepdims=True)
                self.e[k, pl.ds(row, n), cols] = e.astype(jnp.bfloat16)

    def slot_block(self, slot):
        bias = self.bias(slot)
        row = slot * T if isinstance(slot, int) else pl.multiple_of(slot * T, T)
        self.forward(
            lambda k: self.kv[slot, :, pl.ds(pl.multiple_of(k * D, D), D)],
            lambda k: self.kv[slot, :, pl.ds(pl.multiple_of(512 + k * D, D), D)],
            bias,
            row,
            slot,
            T,
        )

    def prompt_block(self):
        self.forward(
            lambda k: self.pg[0, :, pl.ds(pl.multiple_of(k * D, D), D)],
            lambda k: self.pg[1, :, pl.ds(pl.multiple_of(k * D, D), D)],
            None,
            PROMPT,
            17,
            PR,
        )

    def settle(self):
        self.l[...] = 1.0 / self.l[...]
        self.w[...] = self.w[...] * self.l[...]

    def grads(self, k, block, row, n):
        f = jnp.exp2(self.mb[block, k] - self.m[k]) * self.l[k]
        p = self.e[k, pl.ds(row, n), :].astype(jnp.float32) * f
        ds = (p * ((self.dp[k, pl.ds(row, n), :] - self.w[k]) * SCALE)).astype(jnp.bfloat16)
        return p, ds

    def add_dq(self, k, keys, ds):
        self.dq[k] += lax.dot_general(keys, ds, (((0,), (0,)), ((), ())), preferred_element_type=jnp.float32)

    def prompt_grads(self, part):
        @pl.loop(0, KVH)
        def _(k):
            cols = pl.ds(pl.multiple_of(k * D, D), D)
            p, ds = self.grads(k, 17, PROMPT, PR)
            part[0, :, cols] = jnp.dot(ds, self.qn[k], preferred_element_type=jnp.float32)
            part[1, :, cols] = jnp.dot(p.astype(jnp.bfloat16), self.don[k], preferred_element_type=jnp.float32)
            self.add_dq(k, self.pg[0, :, cols], ds)

    def slot_grads(self, slot):
        row = slot * T if isinstance(slot, int) else pl.multiple_of(slot * T, T)

        @pl.loop(0, KVH)
        def _(k):
            _, ds = self.grads(k, slot, row, T)
            self.add_dq(k, self.kv[slot, :, pl.ds(pl.multiple_of(k * D, D), D)], ds)

    def pair_grads(self, pair):
        row = pl.multiple_of(pair * 2 * T, 2 * T)

        @pl.loop(0, KVH)
        def _(k):
            _, d0 = self.grads(k, 2 * pair, row, T)
            _, d1 = self.grads(k, 2 * pair + 1, row + T, T)
            cols = pl.ds(pl.multiple_of(k * D, D), D)
            keys = self.kv[pl.ds(2 * pair, 2), :, cols].reshape(2 * T, D)
            self.add_dq(k, keys, jnp.concatenate([d0, d1], axis=0))

    def store(self, out):
        for k in range(KVH):
            for h in range(QPK):
                hd = k * QPK + h
                out[:, hd * D : (hd + 1) * D] = self.dq[k, :, h * T : (h + 1) * T].T.astype(jnp.bfloat16)


ATTEND_SCRATCH = [
    pltpu.VMEM((KVH, D, G), jnp.bfloat16),
    pltpu.VMEM((KVH, D, G), jnp.bfloat16),
    pltpu.VMEM((KVH, G, D), jnp.bfloat16),
    pltpu.VMEM((KVH, G, D), jnp.bfloat16),
    pltpu.VMEM((KVH, KEYS, G), jnp.bfloat16),
    pltpu.VMEM((KVH, KEYS, G), jnp.float32),
    pltpu.VMEM((KVH, 1, G), jnp.float32),
    pltpu.VMEM((KVH, 1, G), jnp.float32),
    pltpu.VMEM((KVH, 1, G), jnp.float32),
    pltpu.VMEM((18, KVH, 1, G), jnp.float32),
    pltpu.VMEM((KVH, D, G), jnp.float32),
]


def attend_kernel(q, do, kv, pg, lengths, dq, part, *scratch):
    a = Attend(q, do, kv, pg, lengths, scratch)
    a.prepare()
    a.slot_block(OWN)
    a.prompt_block()

    @pl.loop(0, 16)
    def _(slot):
        a.slot_block(slot)

    a.settle()
    a.prompt_grads(part)
    a.slot_grads(OWN)

    @pl.loop(0, 8)
    def _(pair):
        a.pair_grads(pair)

    a.store(dq)


class Reduce:
    def __init__(self, part, ko, vo, sc):
        self.part, self.ko, self.vo = part, ko, vo
        (self.s0, self.r0, self.acc, self.s1, self.r1, self.acc2, self.r2, self.s3, self.r3, self.ss, self.rs) = sc
        self.c, self.r, self.z, self.xy, self.role, self.mate = place()
        self.ylo = self.r // 2

    def peers(self):
        out = [(self.c, self.mate)]
        for s in range(1, NZ):
            out.append((self.xy * NZ + lax.rem(self.z + s, NZ), self.r))
        for s in range(1, 16):
            out.append(self.target(s)[:2])
        return out

    def target(self, s):
        me = self.xy * 2 + self.ylo
        other = lax.rem(me + s, 16)
        return (other // 2) * NZ + self.z, lax.rem(other, 2) * 2 + self.role, other

    def run(self):
        role, z, xy = self.role, self.z, self.xy
        self.s0[...] = self.part[1 - role].astype(jnp.bfloat16)
        first = remote(self.s0, self.r0, self.ss.at[0], self.rs.at[0], self.c, self.mate)
        first.start()
        first.wait_recv()
        for i in range(NXY):
            rows = slice(i * 64, (i + 1) * 64)
            self.acc[i] = (self.part[role, rows, :] + self.r0[rows, :].astype(jnp.float32)).reshape(NZ, 8, 512)
        for i in range(NZ):
            self.s1[i] = self.acc[:, i].reshape(64, 512).astype(jnp.bfloat16)
        copies = []
        for s in range(1, NZ):
            other = lax.rem(z + s, NZ)
            copies.append(
                remote(self.s1.at[other], self.r1.at[s], self.ss.at[s], self.rs.at[s], xy * NZ + other, self.r)
            )
        for copy in copies:
            copy.start()
        total = self.acc[:, z].reshape(64, 512)
        for s, copy in enumerate(copies, 1):
            copy.wait_recv()
            total = total + self.r1[s].astype(jnp.float32)
        self.acc2[...] = total.reshape(NXY, 8, 512)
        second = []
        for s in range(1, 16):
            ctx, resp, other = self.target(s)
            second.append(
                remote(self.acc2.at[other // 2], self.r2.at[s], self.ss.at[8 + s], self.rs.at[8 + s], ctx, resp)
            )
        for copy in second:
            copy.start()
        total = self.acc2[xy]
        for s, copy in enumerate(second, 1):
            copy.wait_recv()
            total = total + self.r2[s]
        self.s3[...] = total
        last = remote(self.s3, self.r3, self.ss.at[8], self.rs.at[8], self.c, self.mate)
        last.start()
        last.wait_recv()
        mine, other = self.s3[...], self.r3[...]
        self.ko[...] = jnp.where(role == 0, mine, other).astype(jnp.bfloat16)
        self.vo[...] = jnp.where(role == 0, other, mine).astype(jnp.bfloat16)
        for copy in [first] + copies + second + [last]:
            copy.wait_send()


REDUCE_SCRATCH = [
    pltpu.VMEM((512, 512), jnp.bfloat16),
    pltpu.VMEM((512, 512), jnp.bfloat16),
    pltpu.VMEM((NXY, NZ, 8, 512), jnp.float32),
    pltpu.VMEM((NZ, 64, 512), jnp.bfloat16),
    pltpu.VMEM((NZ, 64, 512), jnp.bfloat16),
    pltpu.VMEM((NXY, 8, 512), jnp.float32),
    pltpu.VMEM((16, 8, 512), jnp.float32),
    pltpu.VMEM((8, 512), jnp.float32),
    pltpu.VMEM((8, 512), jnp.float32),
    pltpu.SemaphoreType.DMA((24,)),
    pltpu.SemaphoreType.DMA((24,)),
]


def reduce_kernel(part, ko, vo, *scratch):
    r = Reduce(part, ko, vo, scratch)
    greet(r.peers())
    r.run()


VM = pl.BlockSpec(memory_space=pltpu.VMEM)
SM = pl.BlockSpec(memory_space=pltpu.SMEM)
MIB = 2**20


def body(queries, cotangent, sampled_keys, sampled_values, prompt_keys, prompt_values, lengths):
    kv, pg = pl.pallas_call(
        gather_kernel,
        out_shape=(
            jax.ShapeDtypeStruct((17, T, 1024), jnp.bfloat16),
            jax.ShapeDtypeStruct((2, PR, 512), jnp.bfloat16),
        ),
        in_specs=[VM] * 4,
        out_specs=(VM, VM),
        scratch_shapes=[
            pltpu.VMEM((NZ, 8, 512), jnp.float32),
            pltpu.SemaphoreType.DMA((20,)),
            pltpu.SemaphoreType.DMA((17,)),
            pltpu.SemaphoreType.DMA((16,)),
            pltpu.SemaphoreType.DMA((16,)),
        ],
        compiler_params=pltpu.CompilerParams(
            collective_id=0, has_side_effects=True, vmem_limit_bytes=32 * MIB
        ),
        name="gather",
    )(sampled_keys[0], sampled_values[0], prompt_keys, prompt_values)
    dq, part = pl.pallas_call(
        attend_kernel,
        out_shape=(
            jax.ShapeDtypeStruct((T, HQ * D), jnp.bfloat16),
            jax.ShapeDtypeStruct((2, PR, 512), jnp.float32),
        ),
        in_specs=[VM] * 4 + [SM],
        out_specs=(VM, VM),
        scratch_shapes=ATTEND_SCRATCH,
        compiler_params=pltpu.CompilerParams(vmem_limit_bytes=60 * MIB),
        name="attend",
    )(queries[0], cotangent[0], kv, pg, lengths)
    ko, vo = pl.pallas_call(
        reduce_kernel,
        out_shape=(jax.ShapeDtypeStruct((8, 512), jnp.bfloat16),) * 2,
        in_specs=[VM],
        out_specs=(VM, VM),
        scratch_shapes=REDUCE_SCRATCH,
        compiler_params=pltpu.CompilerParams(
            collective_id=1, has_side_effects=True, vmem_limit_bytes=32 * MIB
        ),
        name="reduce",
    )(part)
    return dq[None], ko, vo


def solution(mesh):
    rows = P("resp", "ctx", None)
    in_specs = (rows, rows, rows, rows, P("ctx", None), P("ctx", None), P("resp", None))
    out_specs = (rows, P("ctx", None), P("ctx", None))
    return jax.shard_map(body, mesh=mesh, in_specs=in_specs, out_specs=out_specs, check_vma=False)
```

```python
import jax
import jax.numpy as jnp
from jax import lax
from jax.experimental import pallas as pl
from jax.experimental.pallas import tpu as pltpu
from jax.sharding import PartitionSpec as P

D = 128
KVH = 4
QPK = 5
HQ = KVH * QPK
T = 128
PR = 512
G = QPK * T
NZ = 8
NXY = 8
UP = 4
DOWN = NZ - 1 - UP
SCALE = D ** (-0.5)
LOG2E = 1.4426950408889634
NEG = -1e30
OWN = 16
PROMPT = 17 * T
KEYS = 17 * T + PR
MESH = pl.DeviceIdType.MESH


def remote(src, dst, send, recv, ctx, resp):
    return pltpu.make_async_remote_copy(
        src_ref=src,
        dst_ref=dst,
        send_sem=send,
        recv_sem=recv,
        device_id=(ctx, resp),
        device_id_type=MESH,
    )


def place():
    c = lax.axis_index("ctx")
    r = lax.axis_index("resp")
    z = lax.rem(c, NZ)
    xy = c // NZ
    role = lax.rem(r, 2)
    return c, r, z, xy, role, r + 1 - 2 * role


def greet(peers):
    barrier = pltpu.get_barrier_semaphore()
    for ctx, resp in peers:
        pl.semaphore_signal(barrier, inc=1, device_id=(ctx, resp), device_id_type=MESH)
    pl.semaphore_wait(barrier, len(peers))


class Gather:
    def __init__(self, kv, pg, za, ks, kr, ps, pr):
        self.kv, self.pg, self.za = kv, pg, za
        self.ks, self.kr, self.ps, self.pr = ks, kr, ps, pr
        self.c, self.r, self.z, self.xy, self.role, self.mate = place()

    def peers(self):
        out = []
        for s in range(1, NZ):
            out.append((self.xy * NZ + lax.rem(self.z + s, NZ), self.r))
        for s in range(1, NXY):
            out.append((lax.rem(self.xy + s, NXY) * NZ + self.z, self.r))
        out.append((self.c, self.mate))
        return out

    def piece(self, src, dst, send, ctx):
        return remote(self.kv.at[src], self.kv.at[dst], self.ks.at[send], self.kr.at[dst], ctx, self.r)

    def arrived(self, slot):
        self.piece(slot, slot, slot, self.c).wait_recv()

    def own_sends(self):
        z = self.z
        after = lax.rem(self.c + NZ, NZ * NXY)
        second = lax.rem(self.c + 2 * NZ, NZ * NXY)
        return [
            (None, self.piece(OWN, z, 17, second)),
            (None, self.piece(OWN, 8 + z, 16, after)),
            (z < NZ - 1, self.piece(OWN, z, 18, self.c + 1)),
        ]

    def candidate(self, s, i):
        z = self.z
        low, high = lax.rem(z - s + NZ, NZ), lax.rem(z + s, NZ)
        if i == 0:
            return z >= s, low, True, z < NZ - 1
        if i == 1:
            return (s > 0) & (z + s < NZ), high, False, z > 0
        if i == 2:
            return s <= UP, NZ + low, True, s < UP
        return (s > 0) & (s <= DOWN), NZ + high, False, s < DOWN

    def onward(self, slot, up):
        to = lax.rem(self.z + (1 if up else NZ - 1), NZ)
        return self.piece(slot, slot, slot, self.xy * NZ + to)

    def first_sends(self):
        z = self.z
        up = self.xy * NZ + lax.rem(z + 1, NZ)
        return [
            (z > 0, self.onward(z, False)),
            (None, self.piece(NZ + z, NZ + z, 19, up)),
            (None, self.onward(NZ + z, False)),
        ]

    @staticmethod
    def when(condition, do):
        if condition is None:
            do()
        else:
            pl.when(condition)(do)

    def start_own(self):
        for condition, copy in self.own_sends():
            self.when(condition, copy.start)

    def take_first(self):
        self.arrived(self.z)
        self.arrived(NZ + self.z)
        for condition, copy in self.first_sends():
            self.when(condition, copy.start)

    def take_step(self, s):
        for i in range(4):
            condition, slot, up, more = self.candidate(s, i)

            @pl.when(condition)
            def _(slot=slot, up=up, more=more):
                self.arrived(slot)
                pl.when(more)(self.onward(slot, up).start)

    def finish(self):
        for condition, copy in self.own_sends() + self.first_sends():
            self.when(condition, copy.wait_send)

        @pl.loop(1, NZ)
        def _(s):
            for i in range(4):
                condition, slot, up, more = self.candidate(s, i)
                pl.when(condition & more)(self.onward(slot, up).wait_send)

    def prompt_z(self, pk, pv):
        z = self.z
        mine = jnp.where(self.role == 0, pk[...].astype(jnp.float32), pv[...].astype(jnp.float32))
        self.za[z] = mine
        self.zcopies = [
            remote(
                self.za.at[z],
                self.za.at[z],
                self.ps.at[s],
                self.pr.at[s],
                self.xy * NZ + lax.rem(z + s, NZ),
                self.r,
            )
            for s in range(1, NZ)
        ]
        for copy in self.zcopies:
            copy.start()

    def prompt_xy(self):
        for s, copy in enumerate(self.zcopies, 1):
            source = lax.rem(self.z - s + NZ, NZ)
            remote(self.za.at[source], self.za.at[source], self.ps.at[s], self.pr.at[s], self.c, self.r).wait_recv()
        rows = pl.ds(pl.multiple_of(self.xy * 64, 64), 64)
        self.pg[self.role, rows, :] = self.za[...].reshape(64, 512).astype(jnp.bfloat16)
        self.xycopies = [
            remote(
                self.pg.at[self.role, rows],
                self.pg.at[self.role, rows],
                self.ps.at[8 + s],
                self.pr.at[8 + s],
                lax.rem(self.xy + s, NXY) * NZ + self.z,
                self.r,
            )
            for s in range(1, NXY)
        ]
        for copy in self.xycopies:
            copy.start()

    def prompt_core(self):
        for s in range(1, NXY):
            source = lax.rem(self.xy - s + NXY, NXY)
            rows = pl.ds(pl.multiple_of(source * 64, 64), 64)
            block = self.pg.at[self.role, rows]
            remote(block, block, self.ps.at[8 + s], self.pr.at[8 + s], self.c, self.r).wait_recv()
        half = self.pg.at[self.role]
        self.corecopy = remote(half, half, self.ps.at[0], self.pr.at[0], self.c, self.mate)
        self.corecopy.start()

    def prompt_done(self):
        other = self.pg.at[1 - self.role]
        remote(other, other, self.ps.at[0], self.pr.at[0], self.c, self.mate).wait_recv()

    def prompt_sent(self):
        for copy in self.zcopies + self.xycopies + [self.corecopy]:
            copy.wait_send()


class Attend:
    def __init__(self, q, do, kv, pg, lengths, sc):
        self.q, self.do, self.kv, self.pg, self.lengths = q, do, kv, pg, lengths
        (self.qt, self.dot_, self.qn, self.don, self.e, self.ep, self.dp) = sc[:7]
        (self.m, self.l, self.w, self.mb, self.dq) = sc[7:]

    def prepare(self):
        for k in range(KVH):
            for h in range(QPK):
                cols = slice((k * QPK + h) * D, (k * QPK + h + 1) * D)
                rows = slice(h * T, (h + 1) * T)
                self.qn[k, rows, :] = self.q[:, cols]
                self.don[k, rows, :] = self.do[:, cols]
                self.qt[k, :, rows] = self.q[:, cols].T
                self.dot_[k, :, rows] = self.do[:, cols].T
        self.m[...] = jnp.full(self.m.shape, NEG, jnp.float32)
        self.l[...] = jnp.zeros(self.l.shape, jnp.float32)
        self.w[...] = jnp.zeros(self.w.shape, jnp.float32)
        self.dq[...] = jnp.zeros(self.dq.shape, jnp.float32)
        c = lax.axis_index("ctx")
        self.first = c * T
        self.qpos = self.first + lax.broadcasted_iota(jnp.int32, (1, T), 1)
        start = jnp.zeros((1, T), jnp.int32)
        end = jnp.int32(0)
        for s in range(8):
            end = end + self.lengths[0, s]
            start = jnp.where(self.qpos >= end, end, start)
        self.start = start

    def bias(self, slot):
        c = lax.axis_index("ctx")
        z = lax.rem(c, NZ)
        if isinstance(slot, int) and slot == OWN:
            base = c
        else:
            part = lax.rem(slot, NZ)
            near = c - z + part
            base = jnp.where(slot < NZ, jnp.where(part < z, near, near - 2 * NZ), near - NZ)
        pos = base * T + lax.broadcasted_iota(jnp.int32, (T, T), 0)
        visible = (pos >= self.start) & (pos <= self.qpos)
        return jnp.where(visible, 0.0, NEG).astype(jnp.float32)

    def forward(self, keys, values, bias, row, block, n):
        @pl.loop(0, KVH)
        def _(k):
            s = jnp.dot(keys(k), self.qt[k], preferred_element_type=jnp.float32)
            dp = jnp.dot(values(k), self.dot_[k], preferred_element_type=jnp.float32)
            self.dp[k, pl.ds(row, n), :] = dp
            for h in range(QPK):
                cols = slice(h * T, (h + 1) * T)
                x = s[:, cols] * (SCALE * LOG2E)
                if bias is not None:
                    x = x + bias
                old = self.m[k, :, cols]
                new = jnp.maximum(old, jnp.max(x, axis=0, keepdims=True))
                f = jnp.exp2(old - new)
                e = jnp.exp2(x - new)
                self.m[k, :, cols] = new
                self.mb[block, k, :, cols] = new
                self.l[k, :, cols] = self.l[k, :, cols] * f + jnp.sum(e, axis=0, keepdims=True)
                self.w[k, :, cols] = self.w[k, :, cols] * f + jnp.sum(e * dp[:, cols], axis=0, keepdims=True)
                if bias is None:
                    self.ep[k, pl.ds(row - PROMPT, n), cols] = e
                else:
                    self.e[k, pl.ds(row, n), cols] = e.astype(jnp.bfloat16)

    def slot_block(self, slot):
        bias = self.bias(slot)
        row = slot * T if isinstance(slot, int) else pl.multiple_of(slot * T, T)
        self.forward(
            lambda k: self.kv[slot, :, pl.ds(pl.multiple_of(k * D, D), D)],
            lambda k: self.kv[slot, :, pl.ds(pl.multiple_of(512 + k * D, D), D)],
            bias,
            row,
            slot,
            T,
        )

    def prompt_block(self, i):
        rows = pl.ds(pl.multiple_of(i * T, T), T)
        self.forward(
            lambda k: self.pg[0, rows, pl.ds(pl.multiple_of(k * D, D), D)],
            lambda k: self.pg[1, rows, pl.ds(pl.multiple_of(k * D, D), D)],
            None,
            pl.multiple_of(PROMPT + i * T, T),
            17 + i,
            T,
        )

    def settle(self):
        self.l[...] = 1.0 / self.l[...]
        self.w[...] = self.w[...] * self.l[...]

    def grads(self, k, block, row, e):
        f = jnp.exp2(self.mb[block, k] - self.m[k]) * self.l[k]
        p = e * f
        ds = (p * ((self.dp[k, pl.ds(row, T), :] - self.w[k]) * SCALE)).astype(jnp.bfloat16)
        return p, ds

    def slot_e(self, k, row):
        return self.e[k, pl.ds(row, T), :].astype(jnp.float32)

    def add_dq(self, k, keys, ds):
        self.dq[k] += lax.dot_general(keys, ds, (((0,), (0,)), ((), ())), preferred_element_type=jnp.float32)

    def prompt_grads(self, part):
        @pl.loop(0, KVH)
        def _(k):
            cols = pl.ds(pl.multiple_of(k * D, D), D)
            blocks = []
            for i in range(4):
                rows = slice(i * T, (i + 1) * T)
                p, ds = self.grads(k, 17 + i, PROMPT + i * T, self.ep[k, rows, :])
                blocks.append(ds)
                part[0, rows, cols] = jnp.dot(ds, self.qn[k], preferred_element_type=jnp.float32)
                part[1, rows, cols] = jnp.dot(p.astype(jnp.bfloat16), self.don[k], preferred_element_type=jnp.float32)
            ds = jnp.concatenate(blocks, axis=0)
            self.add_dq(k, self.pg[0, :, cols], ds)

    def slot_grads(self, slot):
        row = slot * T if isinstance(slot, int) else pl.multiple_of(slot * T, T)

        @pl.loop(0, KVH)
        def _(k):
            _, ds = self.grads(k, slot, row, self.slot_e(k, row))
            self.add_dq(k, self.kv[slot, :, pl.ds(pl.multiple_of(k * D, D), D)], ds)

    def pair_grads(self, pair):
        row = pl.multiple_of(pair * 2 * T, 2 * T)

        @pl.loop(0, KVH)
        def _(k):
            _, d0 = self.grads(k, 2 * pair, row, self.slot_e(k, row))
            _, d1 = self.grads(k, 2 * pair + 1, row + T, self.slot_e(k, row + T))
            cols = pl.ds(pl.multiple_of(k * D, D), D)
            keys = self.kv[pl.ds(2 * pair, 2), :, cols].reshape(2 * T, D)
            self.add_dq(k, keys, jnp.concatenate([d0, d1], axis=0))

    def store(self, out):
        for k in range(KVH):
            for h in range(QPK):
                hd = k * QPK + h
                out[:, hd * D : (hd + 1) * D] = self.dq[k, :, h * T : (h + 1) * T].T.astype(jnp.bfloat16)


ATTEND_SCRATCH = [
    pltpu.VMEM((KVH, D, G), jnp.bfloat16),
    pltpu.VMEM((KVH, D, G), jnp.bfloat16),
    pltpu.VMEM((KVH, G, D), jnp.bfloat16),
    pltpu.VMEM((KVH, G, D), jnp.bfloat16),
    pltpu.VMEM((KVH, 17 * T, G), jnp.bfloat16),
    pltpu.VMEM((KVH, PR, G), jnp.float32),
    pltpu.VMEM((KVH, KEYS, G), jnp.float32),
    pltpu.VMEM((KVH, 1, G), jnp.float32),
    pltpu.VMEM((KVH, 1, G), jnp.float32),
    pltpu.VMEM((KVH, 1, G), jnp.float32),
    pltpu.VMEM((21, KVH, 1, G), jnp.float32),
    pltpu.VMEM((KVH, D, G), jnp.float32),
]


class Reduce:
    def __init__(self, part, ko, vo, sc):
        self.part, self.ko, self.vo = part, ko, vo
        (self.s0, self.r0, self.acc, self.s1, self.r1, self.acc2, self.r2, self.s3, self.r3, self.ss, self.rs) = sc
        self.c, self.r, self.z, self.xy, self.role, self.mate = place()
        self.ylo = self.r // 2

    def peers(self):
        out = [(self.c, self.mate)]
        for s in range(1, NZ):
            out.append((self.xy * NZ + lax.rem(self.z + s, NZ), self.r))
        for s in range(1, 16):
            out.append(self.target(s)[:2])
        return out

    def target(self, s):
        me = self.xy * 2 + self.ylo
        other = lax.rem(me + s, 16)
        return (other // 2) * NZ + self.z, lax.rem(other, 2) * 2 + self.role, other

    def core_start(self):
        self.s0[...] = self.part[1 - self.role].astype(jnp.bfloat16)
        self.first = remote(self.s0, self.r0, self.ss.at[0], self.rs.at[0], self.c, self.mate)
        self.first.start()

    def z_start(self):
        z = self.z
        self.first.wait_recv()
        for i in range(NXY):
            rows = slice(i * 64, (i + 1) * 64)
            self.acc[i] = (self.part[self.role, rows, :] + self.r0[rows, :].astype(jnp.float32)).reshape(NZ, 8, 512)
        for i in range(NZ):
            self.s1[i] = self.acc[:, i].reshape(64, 512).astype(jnp.bfloat16)
        self.copies = []
        for s in range(1, NZ):
            other = lax.rem(z + s, NZ)
            self.copies.append(
                remote(self.s1.at[other], self.r1.at[s], self.ss.at[s], self.rs.at[s], self.xy * NZ + other, self.r)
            )
        for copy in self.copies:
            copy.start()

    def ring_start(self):
        total = self.acc[:, self.z].reshape(64, 512)
        for s, copy in enumerate(self.copies, 1):
            copy.wait_recv()
            total = total + self.r1[s].astype(jnp.float32)
        self.acc2[...] = total.reshape(NXY, 8, 512)
        self.second = []
        for s in range(1, 16):
            ctx, resp, other = self.target(s)
            self.second.append(
                remote(self.acc2.at[other // 2], self.r2.at[s], self.ss.at[8 + s], self.rs.at[8 + s], ctx, resp)
            )
        for copy in self.second:
            copy.start()

    def mate_start(self):
        total = self.acc2[self.xy]
        for s, copy in enumerate(self.second, 1):
            copy.wait_recv()
            total = total + self.r2[s]
        self.s3[...] = total
        self.last = remote(self.s3, self.r3, self.ss.at[8], self.rs.at[8], self.c, self.mate)
        self.last.start()

    def finish(self):
        self.last.wait_recv()
        mine, other = self.s3[...], self.r3[...]
        self.ko[...] = jnp.where(self.role == 0, mine, other).astype(jnp.bfloat16)
        self.vo[...] = jnp.where(self.role == 0, other, mine).astype(jnp.bfloat16)
        for copy in [self.first] + self.copies + self.second + [self.last]:
            copy.wait_send()


REDUCE_SCRATCH = [
    pltpu.VMEM((512, 512), jnp.bfloat16),
    pltpu.VMEM((512, 512), jnp.bfloat16),
    pltpu.VMEM((NXY, NZ, 8, 512), jnp.float32),
    pltpu.VMEM((NZ, 64, 512), jnp.bfloat16),
    pltpu.VMEM((NZ, 64, 512), jnp.bfloat16),
    pltpu.VMEM((NXY, 8, 512), jnp.float32),
    pltpu.VMEM((16, 8, 512), jnp.float32),
    pltpu.VMEM((8, 512), jnp.float32),
    pltpu.VMEM((8, 512), jnp.float32),
    pltpu.SemaphoreType.DMA((24,)),
    pltpu.SemaphoreType.DMA((24,)),
]


GATHER_SCRATCH = [
    pltpu.VMEM((17, T, 1024), jnp.bfloat16),
    pltpu.VMEM((2, PR, 512), jnp.bfloat16),
    pltpu.VMEM((NZ, 8, 512), jnp.float32),
    pltpu.SemaphoreType.DMA((20,)),
    pltpu.SemaphoreType.DMA((16,)),
    pltpu.SemaphoreType.DMA((16,)),
    pltpu.SemaphoreType.DMA((16,)),
]
OWN_SCRATCH = [
    pltpu.VMEM((T, HQ * D), jnp.bfloat16),
    pltpu.VMEM((T, HQ * D), jnp.bfloat16),
    pltpu.VMEM((2, PR, 512), jnp.float32),
    pltpu.SemaphoreType.DMA((4,)),
]


def kernel(q_in, do_in, k_in, v_in, pk, pv, lengths, dq, ko, vo, *scratch):
    ng, no, na = len(GATHER_SCRATCH), len(OWN_SCRATCH), len(ATTEND_SCRATCH)
    gather_refs, own_refs = scratch[:ng], scratch[ng : ng + no]
    q, do, part, sems = own_refs
    g = Gather(*gather_refs)
    r = Reduce(part, ko, vo, scratch[ng + no + na :])
    a = Attend(q, do, g.kv, g.pg, lengths, scratch[ng + no : ng + no + na])
    loads = [
        pltpu.make_async_copy(k_in, g.kv.at[OWN, :, pl.ds(0, 512)], sems.at[0]),
        pltpu.make_async_copy(v_in, g.kv.at[OWN, :, pl.ds(512, 512)], sems.at[1]),
        pltpu.make_async_copy(q_in, q, sems.at[2]),
        pltpu.make_async_copy(do_in, do, sems.at[3]),
    ]
    for copy in loads:
        copy.start()
    greet(r.peers())
    g.prompt_z(pk, pv)
    loads[0].wait()
    loads[1].wait()
    g.start_own()
    loads[2].wait()
    loads[3].wait()
    a.prepare()
    g.prompt_xy()
    g.take_first()
    a.slot_block(OWN)
    g.prompt_core()

    @pl.loop(1, NZ + 1)
    def _(s):
        pl.when(s < NZ)(lambda: g.take_step(s))

        @pl.loop(0, 4)
        def _(i):
            choices = [g.candidate(s - 1, j) for j in range(4)]
            present, slot = choices[0][0], choices[0][1]
            for j in range(1, 4):
                present = jnp.where(i == j, choices[j][0].astype(jnp.int32), present.astype(jnp.int32))
                slot = jnp.where(i == j, choices[j][1], slot)
            pl.when(present > 0)(lambda: a.slot_block(slot))

        pl.when(s == 2)(g.prompt_done)
        pl.when((s > 2) & (s < 7))(lambda: a.prompt_block(s - 3))

    a.settle()
    a.prompt_grads(part)
    r.core_start()
    a.slot_grads(OWN)
    r.z_start()

    @pl.loop(0, 5)
    def _(pair):
        a.pair_grads(pair)

    r.ring_start()

    @pl.loop(5, 8)
    def _(pair):
        a.pair_grads(pair)

    r.mate_start()
    a.store(dq)
    r.finish()
    g.prompt_sent()
    g.finish()


VM = pl.BlockSpec(memory_space=pltpu.VMEM)
SM = pl.BlockSpec(memory_space=pltpu.SMEM)
ANY = pl.BlockSpec(memory_space=pl.ANY)
MIB = 2**20


def body(queries, cotangent, sampled_keys, sampled_values, prompt_keys, prompt_values, lengths):
    dq, ko, vo = pl.pallas_call(
        kernel,
        out_shape=(
            jax.ShapeDtypeStruct((T, HQ * D), jnp.bfloat16),
            jax.ShapeDtypeStruct((8, 512), jnp.bfloat16),
            jax.ShapeDtypeStruct((8, 512), jnp.bfloat16),
        ),
        in_specs=[ANY] * 4 + [VM] * 2 + [SM],
        out_specs=(VM, VM, VM),
        scratch_shapes=GATHER_SCRATCH + OWN_SCRATCH + ATTEND_SCRATCH + REDUCE_SCRATCH,
        compiler_params=pltpu.CompilerParams(
            collective_id=0, has_side_effects=True, vmem_limit_bytes=62 * MIB
        ),
        name="shared_prompt_backward",
    )(queries[0], cotangent[0], sampled_keys[0], sampled_values[0], prompt_keys, prompt_values, lengths)
    return dq[None], ko, vo


def solution(mesh):
    rows = P("resp", "ctx", None)
    in_specs = (rows, rows, rows, rows, P("ctx", None), P("ctx", None), P("resp", None))
    out_specs = (rows, P("ctx", None), P("ctx", None))
    return jax.shard_map(body, mesh=mesh, in_specs=in_specs, out_specs=out_specs, check_vma=False)
```

```python
import jax
import jax.numpy as jnp
from jax import lax
from jax.experimental import pallas as pl
from jax.experimental.pallas import tpu as pltpu
from jax.sharding import PartitionSpec as P

D = 128
KVH = 4
QPK = 5
HQ = KVH * QPK
T = 128
PR = 512
G = QPK * T
NZ = 8
NXY = 8
ROUNDS = 6
NONE = 31
FROM_BELOW = (416751103, 216251648, 477602817, 1056210978, 508888131, 1050708068, 1041304709, 35754150)
FROM_ABOVE = (137734463, 181808479, 207008127, 273102239, 241187263, 510853599, 317956127, 1052058880)
FROM_BEFORE = (174130184, 1044482089, 1043472458, 241346667, 1048882316, 412363949, 380022990, 1053210863)
TO_ABOVE = (216251664, 477602832, 1056210992, 508888144, 1050708080, 1041304720, 35754160, 416751103)
TO_BELOW = (1052058896, 137734463, 181808479, 207008127, 273102239, 241187263, 510853599, 317956127)
SCALE = D ** (-0.5)
LOG2E = 1.4426950408889634
NEG = -1e30
OWN = 16
PROMPT = 17 * T
KEYS = 17 * T + PR
MESH = pl.DeviceIdType.MESH


def remote(src, dst, send, recv, ctx, resp):
    return pltpu.make_async_remote_copy(
        src_ref=src,
        dst_ref=dst,
        send_sem=send,
        recv_sem=recv,
        device_id=(ctx, resp),
        device_id_type=MESH,
    )


def place():
    c = lax.axis_index("ctx")
    r = lax.axis_index("resp")
    z = lax.rem(c, NZ)
    xy = c // NZ
    role = lax.rem(r, 2)
    return c, r, z, xy, role, r + 1 - 2 * role


def greet(peers):
    barrier = pltpu.get_barrier_semaphore()
    for ctx, resp in peers:
        pl.semaphore_signal(barrier, inc=1, device_id=(ctx, resp), device_id_type=MESH)
    pl.semaphore_wait(barrier, len(peers))


class Gather:
    def __init__(self, kv, pg, za, ks, kr, ps, pr):
        self.kv, self.pg, self.za = kv, pg, za
        self.ks, self.kr, self.ps, self.pr = ks, kr, ps, pr
        self.c, self.r, self.z, self.xy, self.role, self.mate = place()

    def peers(self):
        out = []
        for s in range(1, NZ):
            out.append((self.xy * NZ + lax.rem(self.z + s, NZ), self.r))
        for s in range(1, NXY):
            out.append((lax.rem(self.xy + s, NXY) * NZ + self.z, self.r))
        out.append((self.c, self.mate))
        return out

    def piece(self, src, dst, send, ctx):
        return remote(self.kv.at[src], self.kv.at[dst], self.ks.at[send], self.kr.at[dst], ctx, self.r)

    def arrived(self, slot):
        self.piece(slot, slot, slot, self.c).wait_recv()

    @staticmethod
    def when(condition, do):
        if condition is None:
            do()
        else:
            pl.when(condition)(do)

    def tables(self):
        def row(table):
            word = self.z * 0
            for i in range(NZ):
                word = word + (self.z == i).astype(jnp.int32) * table[i]
            return word

        return tuple(row(t) for t in (FROM_BELOW, FROM_ABOVE, FROM_BEFORE, TO_ABOVE, TO_BELOW))

    def sends(self, t, words):
        z = self.z
        t = z * 0 + t
        out = []
        for link, (word, by) in enumerate(((words[3], 1), (words[4], NZ - 1))):
            src = lax.rem(word, 32)
            dst = jnp.where(src == OWN, z, src)
            to = self.xy * NZ + lax.rem(z + by, NZ)
            out.append((src != NONE, (jnp.minimum(src, OWN), jnp.minimum(dst, OWN - 1), link * ROUNDS + t, to)))
        dst = lax.rem(words[2], 32)
        earlier = jnp.where(dst == NZ + z, OWN, jnp.where(dst < NZ, dst + NZ, dst - NZ))
        src = jnp.where(t == 1, OWN, earlier)
        to = lax.rem(self.c + NZ * (1 + (t == 1).astype(jnp.int32)), NZ * NXY)
        out.append((dst != NONE, (jnp.minimum(src, OWN), jnp.minimum(dst, OWN - 1), 2 * ROUNDS + t, to)))
        return out

    def start_round(self, t, words):
        for condition, what in self.sends(t, words):
            pl.when(condition)(lambda what=what: self.piece(*what).start())

    def received(self, words):
        return [lax.rem(word, 32) for word in words[:3]]

    def take_round(self, words):
        for slot in self.received(words):
            pl.when(slot != NONE)(lambda slot=slot: self.arrived(slot))

    @staticmethod
    def following(words):
        return tuple(word // 32 for word in words)

    def finish(self, words):
        def one(t, words):
            for condition, what in self.sends(t, words):
                pl.when(condition)(lambda what=what: self.piece(*what).wait_send())
            return self.following(words)

        lax.fori_loop(0, ROUNDS, one, words)

    def prompt_z(self, pk, pv):
        z = self.z
        mine = jnp.where(self.role == 0, pk[...].astype(jnp.float32), pv[...].astype(jnp.float32))
        self.za[z] = mine
        self.zcopies = [
            remote(
                self.za.at[z],
                self.za.at[z],
                self.ps.at[s],
                self.pr.at[s],
                self.xy * NZ + lax.rem(z + s, NZ),
                self.r,
            )
            for s in range(1, NZ)
        ]
        for copy in self.zcopies:
            copy.start()

    def prompt_xy(self):
        for s, copy in enumerate(self.zcopies, 1):
            source = lax.rem(self.z - s + NZ, NZ)
            remote(self.za.at[source], self.za.at[source], self.ps.at[s], self.pr.at[s], self.c, self.r).wait_recv()
        rows = pl.ds(pl.multiple_of(self.xy * 64, 64), 64)
        self.pg[self.role, rows, :] = self.za[...].reshape(64, 512).astype(jnp.bfloat16)
        self.xycopies = [
            remote(
                self.pg.at[self.role, rows],
                self.pg.at[self.role, rows],
                self.ps.at[8 + s],
                self.pr.at[8 + s],
                lax.rem(self.xy + s, NXY) * NZ + self.z,
                self.r,
            )
            for s in range(1, NXY)
        ]
        for copy in self.xycopies:
            copy.start()

    def prompt_core(self):
        for s in range(1, NXY):
            source = lax.rem(self.xy - s + NXY, NXY)
            rows = pl.ds(pl.multiple_of(source * 64, 64), 64)
            block = self.pg.at[self.role, rows]
            remote(block, block, self.ps.at[8 + s], self.pr.at[8 + s], self.c, self.r).wait_recv()
        self.core_copy().start()

    def core_copy(self):
        half = self.pg.at[self.role]
        return remote(half, half, self.ps.at[0], self.pr.at[0], self.c, self.mate)

    def prompt_done(self):
        other = self.pg.at[1 - self.role]
        remote(other, other, self.ps.at[0], self.pr.at[0], self.c, self.mate).wait_recv()

    def prompt_sent(self):
        for copy in self.zcopies + self.xycopies + [self.core_copy()]:
            copy.wait_send()


class Attend:
    def __init__(self, q, do, kv, pg, lengths, sc):
        self.q, self.do, self.kv, self.pg, self.lengths = q, do, kv, pg, lengths
        (self.qt, self.dot_, self.qn, self.don, self.e, self.ep, self.dp) = sc[:7]
        (self.m, self.l, self.w, self.mb, self.dq) = sc[7:]

    def prepare(self):
        for k in range(KVH):
            for h in range(QPK):
                cols = slice((k * QPK + h) * D, (k * QPK + h + 1) * D)
                rows = slice(h * T, (h + 1) * T)
                self.qn[k, rows, :] = self.q[:, cols]
                self.don[k, rows, :] = self.do[:, cols]
                self.qt[k, :, rows] = self.q[:, cols].T
                self.dot_[k, :, rows] = self.do[:, cols].T
        self.m[...] = jnp.full(self.m.shape, NEG, jnp.float32)
        self.l[...] = jnp.zeros(self.l.shape, jnp.float32)
        self.w[...] = jnp.zeros(self.w.shape, jnp.float32)
        self.dq[...] = jnp.zeros(self.dq.shape, jnp.float32)
        c = lax.axis_index("ctx")
        self.first = c * T
        self.qpos = self.first + lax.broadcasted_iota(jnp.int32, (1, T), 1)
        start = jnp.zeros((1, T), jnp.int32)
        end = jnp.int32(0)
        for s in range(8):
            end = end + self.lengths[0, s]
            start = jnp.where(self.qpos >= end, end, start)
        self.start = start

    def bias(self, slot):
        c = lax.axis_index("ctx")
        z = lax.rem(c, NZ)
        if isinstance(slot, int) and slot == OWN:
            base = c
        else:
            part = lax.rem(slot, NZ)
            near = c - z + part
            base = jnp.where(slot < NZ, jnp.where(part < z, near, near - 2 * NZ), near - NZ)
        pos = base * T + lax.broadcasted_iota(jnp.int32, (T, T), 0)
        visible = (pos >= self.start) & (pos <= self.qpos)
        return jnp.where(visible, 0.0, NEG).astype(jnp.float32)

    def forward(self, keys, values, bias, row, block, n):
        @pl.loop(0, KVH)
        def _(k):
            s = jnp.dot(keys(k), self.qt[k], preferred_element_type=jnp.float32)
            dp = jnp.dot(values(k), self.dot_[k], preferred_element_type=jnp.float32)
            self.dp[k, pl.ds(row, n), :] = dp
            for h in range(QPK):
                cols = slice(h * T, (h + 1) * T)
                x = s[:, cols] * (SCALE * LOG2E)
                if bias is not None:
                    x = x + bias
                old = self.m[k, :, cols]
                new = jnp.maximum(old, jnp.max(x, axis=0, keepdims=True))
                f = jnp.exp2(old - new)
                e = jnp.exp2(x - new)
                self.m[k, :, cols] = new
                self.mb[block, k, :, cols] = new
                self.l[k, :, cols] = self.l[k, :, cols] * f + jnp.sum(e, axis=0, keepdims=True)
                self.w[k, :, cols] = self.w[k, :, cols] * f + jnp.sum(e * dp[:, cols], axis=0, keepdims=True)
                if bias is None:
                    self.ep[k, pl.ds(row - PROMPT, n), cols] = e
                else:
                    self.e[k, pl.ds(row, n), cols] = e.astype(jnp.bfloat16)

    def slot_block(self, slot):
        bias = self.bias(slot)
        row = slot * T if isinstance(slot, int) else pl.multiple_of(slot * T, T)
        self.forward(
            lambda k: self.kv[slot, :, pl.ds(pl.multiple_of(k * D, D), D)],
            lambda k: self.kv[slot, :, pl.ds(pl.multiple_of(512 + k * D, D), D)],
            bias,
            row,
            slot,
            T,
        )

    def prompt_block(self, i):
        rows = pl.ds(pl.multiple_of(i * T, T), T)
        self.forward(
            lambda k: self.pg[0, rows, pl.ds(pl.multiple_of(k * D, D), D)],
            lambda k: self.pg[1, rows, pl.ds(pl.multiple_of(k * D, D), D)],
            None,
            pl.multiple_of(PROMPT + i * T, T),
            17 + i,
            T,
        )

    def settle(self):
        self.l[...] = 1.0 / self.l[...]
        self.w[...] = self.w[...] * self.l[...]

    def grads(self, k, block, row, e):
        f = jnp.exp2(self.mb[block, k] - self.m[k]) * self.l[k]
        p = e * f
        ds = (p * ((self.dp[k, pl.ds(row, T), :] - self.w[k]) * SCALE)).astype(jnp.bfloat16)
        return p, ds

    def slot_e(self, k, row):
        return self.e[k, pl.ds(row, T), :].astype(jnp.float32)

    def add_dq(self, k, keys, ds):
        self.dq[k] += lax.dot_general(keys, ds, (((0,), (0,)), ((), ())), preferred_element_type=jnp.float32)

    def prompt_grads(self, part):
        @pl.loop(0, KVH)
        def _(k):
            cols = pl.ds(pl.multiple_of(k * D, D), D)
            blocks = []
            for i in range(4):
                rows = slice(i * T, (i + 1) * T)
                p, ds = self.grads(k, 17 + i, PROMPT + i * T, self.ep[k, rows, :])
                blocks.append(ds)
                part[0, rows, cols] = jnp.dot(ds, self.qn[k], preferred_element_type=jnp.float32)
                part[1, rows, cols] = jnp.dot(p.astype(jnp.bfloat16), self.don[k], preferred_element_type=jnp.float32)
            ds = jnp.concatenate(blocks, axis=0)
            self.add_dq(k, self.pg[0, :, cols], ds)

    def slot_grads(self, slot):
        row = slot * T if isinstance(slot, int) else pl.multiple_of(slot * T, T)

        @pl.loop(0, KVH)
        def _(k):
            _, ds = self.grads(k, slot, row, self.slot_e(k, row))
            self.add_dq(k, self.kv[slot, :, pl.ds(pl.multiple_of(k * D, D), D)], ds)

    def pair_grads(self, pair):
        row = pl.multiple_of(pair * 2 * T, 2 * T)

        @pl.loop(0, KVH)
        def _(k):
            _, d0 = self.grads(k, 2 * pair, row, self.slot_e(k, row))
            _, d1 = self.grads(k, 2 * pair + 1, row + T, self.slot_e(k, row + T))
            cols = pl.ds(pl.multiple_of(k * D, D), D)
            keys = self.kv[pl.ds(2 * pair, 2), :, cols].reshape(2 * T, D)
            self.add_dq(k, keys, jnp.concatenate([d0, d1], axis=0))

    def store(self, out):
        for k in range(KVH):
            for h in range(QPK):
                hd = k * QPK + h
                out[:, hd * D : (hd + 1) * D] = self.dq[k, :, h * T : (h + 1) * T].T.astype(jnp.bfloat16)


ATTEND_SCRATCH = [
    pltpu.VMEM((KVH, D, G), jnp.bfloat16),
    pltpu.VMEM((KVH, D, G), jnp.bfloat16),
    pltpu.VMEM((KVH, G, D), jnp.bfloat16),
    pltpu.VMEM((KVH, G, D), jnp.bfloat16),
    pltpu.VMEM((KVH, 17 * T, G), jnp.bfloat16),
    pltpu.VMEM((KVH, PR, G), jnp.float32),
    pltpu.VMEM((KVH, KEYS, G), jnp.float32),
    pltpu.VMEM((KVH, 1, G), jnp.float32),
    pltpu.VMEM((KVH, 1, G), jnp.float32),
    pltpu.VMEM((KVH, 1, G), jnp.float32),
    pltpu.VMEM((21, KVH, 1, G), jnp.float32),
    pltpu.VMEM((KVH, D, G), jnp.float32),
]


class Reduce:
    def __init__(self, part, ko, vo, sc):
        self.part, self.ko, self.vo = part, ko, vo
        (self.s0, self.r0, self.acc, self.s1, self.r1, self.acc2, self.r2, self.s3, self.r3, self.ss, self.rs) = sc
        self.c, self.r, self.z, self.xy, self.role, self.mate = place()
        self.ylo = self.r // 2

    def peers(self):
        out = [(self.c, self.mate)]
        for s in range(1, NZ):
            out.append((self.xy * NZ + lax.rem(self.z + s, NZ), self.r))
        for s in range(1, 16):
            out.append(self.target(s)[:2])
        return out

    def target(self, s):
        me = self.xy * 2 + self.ylo
        other = lax.rem(me + s, 16)
        return (other // 2) * NZ + self.z, lax.rem(other, 2) * 2 + self.role, other

    def core_start(self):
        self.s0[...] = self.part[1 - self.role].astype(jnp.bfloat16)
        self.first = remote(self.s0, self.r0, self.ss.at[0], self.rs.at[0], self.c, self.mate)
        self.first.start()

    def z_start(self):
        z = self.z
        self.first.wait_recv()
        for i in range(NXY):
            rows = slice(i * 64, (i + 1) * 64)
            self.acc[i] = (self.part[self.role, rows, :] + self.r0[rows, :].astype(jnp.float32)).reshape(NZ, 8, 512)
        for i in range(NZ):
            self.s1[i] = self.acc[:, i].reshape(64, 512).astype(jnp.bfloat16)
        self.copies = []
        for s in range(1, NZ):
            other = lax.rem(z + s, NZ)
            self.copies.append(
                remote(self.s1.at[other], self.r1.at[s], self.ss.at[s], self.rs.at[s], self.xy * NZ + other, self.r)
            )
        for copy in self.copies:
            copy.start()

    def ring_start(self):
        total = self.acc[:, self.z].reshape(64, 512)
        for s, copy in enumerate(self.copies, 1):
            copy.wait_recv()
            total = total + self.r1[s].astype(jnp.float32)
        self.acc2[...] = total.reshape(NXY, 8, 512)
        self.second = []
        for s in range(1, 16):
            ctx, resp, other = self.target(s)
            self.second.append(
                remote(self.acc2.at[other // 2], self.r2.at[s], self.ss.at[8 + s], self.rs.at[8 + s], ctx, resp)
            )
        for copy in self.second:
            copy.start()

    def mate_start(self):
        total = self.acc2[self.xy]
        for s, copy in enumerate(self.second, 1):
            copy.wait_recv()
            total = total + self.r2[s]
        self.s3[...] = total
        self.last = remote(self.s3, self.r3, self.ss.at[8], self.rs.at[8], self.c, self.mate)
        self.last.start()

    def finish(self):
        self.last.wait_recv()
        mine, other = self.s3[...], self.r3[...]
        self.ko[...] = jnp.where(self.role == 0, mine, other).astype(jnp.bfloat16)
        self.vo[...] = jnp.where(self.role == 0, other, mine).astype(jnp.bfloat16)
        for copy in [self.first] + self.copies + self.second + [self.last]:
            copy.wait_send()


REDUCE_SCRATCH = [
    pltpu.VMEM((512, 512), jnp.bfloat16),
    pltpu.VMEM((512, 512), jnp.bfloat16),
    pltpu.VMEM((NXY, NZ, 8, 512), jnp.float32),
    pltpu.VMEM((NZ, 64, 512), jnp.bfloat16),
    pltpu.VMEM((NZ, 64, 512), jnp.bfloat16),
    pltpu.VMEM((NXY, 8, 512), jnp.float32),
    pltpu.VMEM((16, 8, 512), jnp.float32),
    pltpu.VMEM((8, 512), jnp.float32),
    pltpu.VMEM((8, 512), jnp.float32),
    pltpu.SemaphoreType.DMA((24,)),
    pltpu.SemaphoreType.DMA((24,)),
]


GATHER_SCRATCH = [
    pltpu.VMEM((17, T, 1024), jnp.bfloat16),
    pltpu.VMEM((2, PR, 512), jnp.bfloat16),
    pltpu.VMEM((NZ, 8, 512), jnp.float32),
    pltpu.SemaphoreType.DMA((3 * ROUNDS,)),
    pltpu.SemaphoreType.DMA((16,)),
    pltpu.SemaphoreType.DMA((16,)),
    pltpu.SemaphoreType.DMA((16,)),
]
OWN_SCRATCH = [
    pltpu.VMEM((T, HQ * D), jnp.bfloat16),
    pltpu.VMEM((T, HQ * D), jnp.bfloat16),
    pltpu.VMEM((2, PR, 512), jnp.float32),
    pltpu.SemaphoreType.DMA((4,)),
]


def kernel(q_in, do_in, k_in, v_in, pk, pv, lengths, dq, ko, vo, *scratch):
    ng, no, na = len(GATHER_SCRATCH), len(OWN_SCRATCH), len(ATTEND_SCRATCH)
    gather_refs, own_refs = scratch[:ng], scratch[ng : ng + no]
    q, do, part, sems = own_refs
    g = Gather(*gather_refs)
    r = Reduce(part, ko, vo, scratch[ng + no + na :])
    a = Attend(q, do, g.kv, g.pg, lengths, scratch[ng + no : ng + no + na])
    loads = [
        pltpu.make_async_copy(k_in, g.kv.at[OWN, :, pl.ds(0, 512)], sems.at[0]),
        pltpu.make_async_copy(v_in, g.kv.at[OWN, :, pl.ds(512, 512)], sems.at[1]),
        pltpu.make_async_copy(q_in, q, sems.at[2]),
        pltpu.make_async_copy(do_in, do, sems.at[3]),
    ]
    for copy in loads:
        copy.start()
    greet(r.peers())
    g.prompt_z(pk, pv)
    loads[0].wait()
    loads[1].wait()
    words = g.tables()
    g.start_round(0, words)
    loads[2].wait()
    loads[3].wait()
    a.prepare()
    a.slot_block(OWN)
    g.prompt_xy()

    def one_round(t, words):
        later = g.following(words)
        g.take_round(words)
        pl.when(t < ROUNDS)(lambda: g.start_round(t, later))
        slots = g.received(words)

        @pl.loop(0, 3)
        def _(i):
            slot = jnp.where(i == 0, slots[0], jnp.where(i == 1, slots[1], slots[2]))
            pl.when(slot != NONE)(lambda: a.slot_block(slot))

        pl.when(t == 2)(g.prompt_core)
        pl.when(t == 3)(g.prompt_done)
        low = jnp.minimum(jnp.maximum(t - 3, 0), 2) + 2 * (t // ROUNDS)
        high = jnp.maximum(t - 2, 0) + t // 5 - t // ROUNDS

        @pl.loop(0, 2)
        def _(i):
            pl.when(low + i < high)(lambda: a.prompt_block(low + i))

        return later

    lax.fori_loop(1, ROUNDS + 1, one_round, words)
    a.settle()
    a.prompt_grads(part)
    r.core_start()
    a.slot_grads(OWN)
    r.z_start()

    @pl.loop(0, 5)
    def _(pair):
        a.pair_grads(pair)

    r.ring_start()

    @pl.loop(5, 8)
    def _(pair):
        a.pair_grads(pair)

    r.mate_start()
    a.store(dq)
    r.finish()
    g.prompt_sent()
    g.finish(words)


VM = pl.BlockSpec(memory_space=pltpu.VMEM)
SM = pl.BlockSpec(memory_space=pltpu.SMEM)
ANY = pl.BlockSpec(memory_space=pl.ANY)
MIB = 2**20


def body(queries, cotangent, sampled_keys, sampled_values, prompt_keys, prompt_values, lengths):
    dq, ko, vo = pl.pallas_call(
        kernel,
        out_shape=(
            jax.ShapeDtypeStruct((T, HQ * D), jnp.bfloat16),
            jax.ShapeDtypeStruct((8, 512), jnp.bfloat16),
            jax.ShapeDtypeStruct((8, 512), jnp.bfloat16),
        ),
        in_specs=[ANY] * 4 + [VM] * 2 + [SM],
        out_specs=(VM, VM, VM),
        scratch_shapes=GATHER_SCRATCH + OWN_SCRATCH + ATTEND_SCRATCH + REDUCE_SCRATCH,
        compiler_params=pltpu.CompilerParams(
            collective_id=0, has_side_effects=True, vmem_limit_bytes=62 * MIB
        ),
        name="shared_prompt_backward",
    )(queries[0], cotangent[0], sampled_keys[0], sampled_values[0], prompt_keys, prompt_values, lengths)
    return dq[None], ko, vo


def solution(mesh):
    rows = P("resp", "ctx", None)
    in_specs = (rows, rows, rows, rows, P("ctx", None), P("ctx", None), P("resp", None))
    out_specs = (rows, P("ctx", None), P("ctx", None))
    return jax.shard_map(body, mesh=mesh, in_specs=in_specs, out_specs=out_specs, check_vma=False)
```

```python
import jax
import jax.numpy as jnp
from jax import lax
from jax.experimental import pallas as pl
from jax.experimental.pallas import tpu as pltpu
from jax.sharding import PartitionSpec as P

D = 128
KVH = 4
QPK = 5
HQ = KVH * QPK
T = 128
PR = 512
G = QPK * T
NZ = 8
NXY = 8
ROUNDS = 6
NONE = 31
FROM_BELOW = (416751103, 216251648, 477602817, 1056210978, 508888131, 1050708068, 1041304709, 35754150)
FROM_ABOVE = (137734463, 181808479, 207008127, 273102239, 241187263, 510853599, 317956127, 1052058880)
FROM_BEFORE = (174130184, 1044482089, 1043472458, 241346667, 1048882316, 412363949, 380022990, 1053210863)
TO_ABOVE = (216251664, 477602832, 1056210992, 508888144, 1050708080, 1041304720, 35754160, 416751103)
TO_BELOW = (1052058896, 137734463, 181808479, 207008127, 273102239, 241187263, 510853599, 317956127)
SCALE = D ** (-0.5)
LOG2E = 1.4426950408889634
NEG = -1e30
OWN = 16
PROMPT = 17 * T
KEYS = 17 * T + PR
MESH = pl.DeviceIdType.MESH


def remote(src, dst, send, recv, ctx, resp):
    return pltpu.make_async_remote_copy(
        src_ref=src,
        dst_ref=dst,
        send_sem=send,
        recv_sem=recv,
        device_id=(ctx, resp),
        device_id_type=MESH,
    )


def place():
    c = lax.axis_index("ctx")
    r = lax.axis_index("resp")
    z = lax.rem(c, NZ)
    xy = c // NZ
    role = lax.rem(r, 2)
    return c, r, z, xy, role, r + 1 - 2 * role


def greet(peers):
    barrier = pltpu.get_barrier_semaphore()
    for ctx, resp in peers:
        pl.semaphore_signal(barrier, inc=1, device_id=(ctx, resp), device_id_type=MESH)
    return barrier, len(peers)


class Gather:
    def __init__(self, kv, pg, za, ks, kr, ps, pr):
        self.kv, self.pg, self.za = kv, pg, za
        self.ks, self.kr, self.ps, self.pr = ks, kr, ps, pr
        self.c, self.r, self.z, self.xy, self.role, self.mate = place()

    def peers(self):
        out = []
        for s in range(1, NZ):
            out.append((self.xy * NZ + lax.rem(self.z + s, NZ), self.r))
        for s in range(1, NXY):
            out.append((lax.rem(self.xy + s, NXY) * NZ + self.z, self.r))
        out.append((self.c, self.mate))
        return out

    def piece(self, half, src, dst, send, ctx):
        return remote(
            self.kv.at[half, src],
            self.kv.at[half, dst],
            self.ks.at[half * 3 * ROUNDS + send],
            self.kr.at[half * OWN + dst],
            ctx,
            self.r,
        )

    def arrived(self, half, slot):
        self.piece(half, slot, slot, 0, self.c).wait_recv()

    @staticmethod
    def when(condition, do):
        if condition is None:
            do()
        else:
            pl.when(condition)(do)

    def tables(self):
        def row(table):
            word = self.z * 0
            for i in range(NZ):
                word = word + (self.z == i).astype(jnp.int32) * table[i]
            return word

        return tuple(row(t) for t in (FROM_BELOW, FROM_ABOVE, FROM_BEFORE, TO_ABOVE, TO_BELOW))

    def sends(self, t, words):
        z = self.z
        t = z * 0 + t
        out = []
        for link, (word, by) in enumerate(((words[3], 1), (words[4], NZ - 1))):
            src = lax.rem(word, 32)
            dst = jnp.where(src == OWN, z, src)
            to = self.xy * NZ + lax.rem(z + by, NZ)
            out.append((src != NONE, (jnp.minimum(src, OWN), jnp.minimum(dst, OWN - 1), link * ROUNDS + t, to)))
        dst = lax.rem(words[2], 32)
        earlier = jnp.where(dst == NZ + z, OWN, jnp.where(dst < NZ, dst + NZ, dst - NZ))
        src = jnp.where(t == 1, OWN, earlier)
        to = lax.rem(self.c + NZ * (1 + (t == 1).astype(jnp.int32)), NZ * NXY)
        out.append((dst != NONE, (jnp.minimum(src, OWN), jnp.minimum(dst, OWN - 1), 2 * ROUNDS + t, to)))
        return out

    def start_round(self, half, t, words):
        for condition, what in self.sends(t, words):
            pl.when(condition)(lambda what=what: self.piece(half, *what).start())

    def received(self, words):
        return [lax.rem(word, 32) for word in words[:3]]

    def take_round(self, half, words):
        for slot in self.received(words):
            pl.when(slot != NONE)(lambda slot=slot: self.arrived(half, slot))

    @staticmethod
    def following(words):
        return tuple(word // 32 for word in words)

    def finish(self, words):
        def one(t, words):
            for condition, what in self.sends(t, words):
                for half in range(2):
                    pl.when(condition)(lambda half=half, what=what: self.piece(half, *what).wait_send())
            return self.following(words)

        lax.fori_loop(0, ROUNDS, one, words)

    def prompt_z(self, pk, pv):
        z = self.z
        mine = jnp.where(self.role == 0, pk[...].astype(jnp.float32), pv[...].astype(jnp.float32))
        self.za[z] = mine
        self.zcopies = [
            remote(
                self.za.at[z],
                self.za.at[z],
                self.ps.at[s],
                self.pr.at[s],
                self.xy * NZ + lax.rem(z + s, NZ),
                self.r,
            )
            for s in range(1, NZ)
        ]
        for copy in self.zcopies:
            copy.start()

    def prompt_pair(self):
        for s in range(1, NZ):
            source = lax.rem(self.z - s + NZ, NZ)
            remote(self.za.at[source], self.za.at[source], self.ps.at[s], self.pr.at[s], self.c, self.r).wait_recv()
        rows = pl.ds(pl.multiple_of(self.xy * 64, 64), 64)
        self.pg[self.role, rows, :] = self.za[...].reshape(64, 512).astype(jnp.bfloat16)
        self.pair_copy(self.xy).start()

    def pair_copy(self, xy):
        block = self.pg.at[self.role, pl.ds(pl.multiple_of(xy * 64, 64), 64)]
        to = self.xy + 1 - 2 * lax.rem(self.xy, 2)
        return remote(block, block, self.ps.at[8], self.pr.at[8], to * NZ + self.z, self.r)

    def x_copy(self, k):
        x = lax.rem(self.xy // 2 + k, 4)
        block = self.pg.at[self.role, pl.ds(pl.multiple_of(x * 128, 128), 128)]
        to = lax.rem(self.c + 6 * NZ, NXY * NZ)
        return remote(block, block, self.ps.at[9 + k], self.pr.at[9 + k], to, self.r)

    def prompt_hop(self, k):
        if k == 0:
            self.pair_copy(self.xy + 1 - 2 * lax.rem(self.xy, 2)).wait_recv()
        else:
            x = lax.rem(self.xy // 2 + k, 4)
            block = self.pg.at[self.role, pl.ds(pl.multiple_of(x * 128, 128), 128)]
            remote(block, block, self.ps.at[8 + k], self.pr.at[8 + k], self.c, self.r).wait_recv()
        if k < 3:
            self.x_copy(k).start()
        else:
            self.core_copy().start()

    def core_copy(self):
        half = self.pg.at[self.role]
        return remote(half, half, self.ps.at[0], self.pr.at[0], self.c, self.mate)

    def prompt_done(self):
        other = self.pg.at[1 - self.role]
        remote(other, other, self.ps.at[0], self.pr.at[0], self.c, self.mate).wait_recv()

    def prompt_sent(self):
        for copy in self.zcopies + [self.pair_copy(self.xy)] + [self.x_copy(k) for k in range(3)] + [self.core_copy()]:
            copy.wait_send()


class Attend:
    def __init__(self, q, do, kv, pg, lengths, sc):
        self.q, self.do, self.kv, self.pg, self.lengths = q, do, kv, pg, lengths
        (self.qt, self.dot_, self.qn, self.don, self.e, self.ep, self.dp) = sc[:7]
        (self.m, self.l, self.w, self.mb, self.dq) = sc[7:]

    def prepare(self):
        for k in range(KVH):
            for h in range(QPK):
                cols = slice((k * QPK + h) * D, (k * QPK + h + 1) * D)
                rows = slice(h * T, (h + 1) * T)
                self.qn[k, rows, :] = self.q[:, cols]
                self.don[k, rows, :] = self.do[:, cols]
                self.qt[k, :, rows] = self.q[:, cols].T
                self.dot_[k, :, rows] = self.do[:, cols].T
        self.m[...] = jnp.full(self.m.shape, NEG, jnp.float32)
        self.l[...] = jnp.zeros(self.l.shape, jnp.float32)
        self.w[...] = jnp.zeros(self.w.shape, jnp.float32)
        self.dq[...] = jnp.zeros(self.dq.shape, jnp.float32)
        c = lax.axis_index("ctx")
        self.first = c * T
        self.qpos = self.first + lax.broadcasted_iota(jnp.int32, (1, T), 1)
        start = jnp.zeros((1, T), jnp.int32)
        end = jnp.int32(0)
        for s in range(8):
            end = end + self.lengths[0, s]
            start = jnp.where(self.qpos >= end, end, start)
        self.start = start

    def bias(self, slot):
        c = lax.axis_index("ctx")
        z = lax.rem(c, NZ)
        if isinstance(slot, int) and slot == OWN:
            base = c
        else:
            part = lax.rem(slot, NZ)
            near = c - z + part
            base = jnp.where(slot < NZ, jnp.where(part < z, near, near - 2 * NZ), near - NZ)
        pos = base * T + lax.broadcasted_iota(jnp.int32, (T, T), 0)
        visible = (pos >= self.start) & (pos <= self.qpos)
        return jnp.where(visible, 0.0, NEG).astype(jnp.float32)

    def forward(self, keys, values, bias, row, block, n):
        @pl.loop(0, KVH)
        def _(k):
            s = jnp.dot(keys(k), self.qt[k], preferred_element_type=jnp.float32)
            dp = jnp.dot(values(k), self.dot_[k], preferred_element_type=jnp.float32)
            self.dp[k, pl.ds(row, n), :] = dp
            for h in range(QPK):
                cols = slice(h * T, (h + 1) * T)
                x = s[:, cols] * (SCALE * LOG2E)
                if bias is not None:
                    x = x + bias
                old = self.m[k, :, cols]
                new = jnp.maximum(old, jnp.max(x, axis=0, keepdims=True))
                f = jnp.exp2(old - new)
                e = jnp.exp2(x - new)
                self.m[k, :, cols] = new
                self.mb[block, k, :, cols] = new
                self.l[k, :, cols] = self.l[k, :, cols] * f + jnp.sum(e, axis=0, keepdims=True)
                self.w[k, :, cols] = self.w[k, :, cols] * f + jnp.sum(e * dp[:, cols], axis=0, keepdims=True)
                if bias is None:
                    self.ep[k, pl.ds(row - PROMPT, n), cols] = e
                else:
                    self.e[k, pl.ds(row, n), cols] = e.astype(jnp.bfloat16)

    def slot_block(self, slot):
        bias = self.bias(slot)
        row = slot * T if isinstance(slot, int) else pl.multiple_of(slot * T, T)
        self.forward(
            lambda k: self.kv[0, slot, :, pl.ds(pl.multiple_of(k * D, D), D)],
            lambda k: self.kv[1, slot, :, pl.ds(pl.multiple_of(k * D, D), D)],
            bias,
            row,
            slot,
            T,
        )

    def prompt_block(self, i):
        rows = pl.ds(pl.multiple_of(i * T, T), T)
        self.forward(
            lambda k: self.pg[0, rows, pl.ds(pl.multiple_of(k * D, D), D)],
            lambda k: self.pg[1, rows, pl.ds(pl.multiple_of(k * D, D), D)],
            None,
            pl.multiple_of(PROMPT + i * T, T),
            17 + i,
            T,
        )

    def settle(self):
        self.l[...] = 1.0 / self.l[...]
        self.w[...] = self.w[...] * self.l[...]

    def grads(self, k, block, row, e):
        f = jnp.exp2(self.mb[block, k] - self.m[k]) * self.l[k]
        p = e * f
        ds = (p * ((self.dp[k, pl.ds(row, T), :] - self.w[k]) * SCALE)).astype(jnp.bfloat16)
        return p, ds

    def slot_e(self, k, row):
        return self.e[k, pl.ds(row, T), :].astype(jnp.float32)

    def add_dq(self, k, keys, ds):
        self.dq[k] += lax.dot_general(keys, ds, (((0,), (0,)), ((), ())), preferred_element_type=jnp.float32)

    def prompt_grads(self, part, ready):
        @pl.loop(0, KVH)
        def _(k):
            cols = pl.ds(pl.multiple_of(k * D, D), D)
            for i in range(4):
                rows = slice(i * T, (i + 1) * T)
                p, ds = self.grads(k, 17 + i, PROMPT + i * T, self.ep[k, rows, :])
                self.ep[k, rows, :] = ds.astype(jnp.float32)
                part[0, rows, cols] = jnp.dot(ds, self.qn[k], preferred_element_type=jnp.float32)
                part[1, rows, cols] = jnp.dot(p.astype(jnp.bfloat16), self.don[k], preferred_element_type=jnp.float32)
            ready(k, cols)

    def prompt_dq(self):
        @pl.loop(0, KVH)
        def _(k):
            cols = pl.ds(pl.multiple_of(k * D, D), D)
            self.add_dq(k, self.pg[0, :, cols], self.ep[k].astype(jnp.bfloat16))

    def slot_grads(self, slot):
        row = slot * T if isinstance(slot, int) else pl.multiple_of(slot * T, T)

        @pl.loop(0, KVH)
        def _(k):
            _, ds = self.grads(k, slot, row, self.slot_e(k, row))
            self.add_dq(k, self.kv[0, slot, :, pl.ds(pl.multiple_of(k * D, D), D)], ds)

    def pair_grads(self, pair):
        row = pl.multiple_of(pair * 2 * T, 2 * T)

        @pl.loop(0, KVH)
        def _(k):
            _, d0 = self.grads(k, 2 * pair, row, self.slot_e(k, row))
            _, d1 = self.grads(k, 2 * pair + 1, row + T, self.slot_e(k, row + T))
            cols = pl.ds(pl.multiple_of(k * D, D), D)
            keys = self.kv[0, pl.ds(2 * pair, 2), :, cols].reshape(2 * T, D)
            self.add_dq(k, keys, jnp.concatenate([d0, d1], axis=0))

    def store(self, out):
        for k in range(KVH):
            for h in range(QPK):
                hd = k * QPK + h
                out[:, hd * D : (hd + 1) * D] = self.dq[k, :, h * T : (h + 1) * T].T.astype(jnp.bfloat16)


ATTEND_SCRATCH = [
    pltpu.VMEM((KVH, D, G), jnp.bfloat16),
    pltpu.VMEM((KVH, D, G), jnp.bfloat16),
    pltpu.VMEM((KVH, G, D), jnp.bfloat16),
    pltpu.VMEM((KVH, G, D), jnp.bfloat16),
    pltpu.VMEM((KVH, 17 * T, G), jnp.bfloat16),
    pltpu.VMEM((KVH, PR, G), jnp.float32),
    pltpu.VMEM((KVH, KEYS, G), jnp.float32),
    pltpu.VMEM((KVH, 1, G), jnp.float32),
    pltpu.VMEM((KVH, 1, G), jnp.float32),
    pltpu.VMEM((KVH, 1, G), jnp.float32),
    pltpu.VMEM((21, KVH, 1, G), jnp.float32),
    pltpu.VMEM((KVH, D, G), jnp.float32),
]


class Reduce:
    def __init__(self, part, ko, vo, sc):
        self.part, self.ko, self.vo = part, ko, vo
        (self.s0, self.r0, self.acc, self.s1, self.r1, self.acc2, self.r2, self.s3, self.r3) = sc[:9]
        self.ss, self.rs, self.zs, self.zr = sc[9:]
        self.c, self.r, self.z, self.xy, self.role, self.mate = place()
        self.ylo = self.r // 2
        self.other_y = (1 - self.ylo) * 2 + self.role

    def peers(self):
        out = [(self.c, self.mate)]
        for s in range(1, NZ):
            ctx = self.xy * NZ + lax.rem(self.z + s, NZ)
            out += [(ctx, self.r), (ctx, self.other_y)]
        for s in range(1, 16):
            out.append(self.target(s)[:2])
        return out

    def target(self, s):
        me = self.xy * 2 + self.ylo
        other = lax.rem(me + s, 16)
        return (other // 2) * NZ + self.z, lax.rem(other, 2) * 2 + self.role, other

    def core_copy(self, k):
        return remote(self.s0.at[k], self.r0.at[k], self.ss.at[k], self.rs.at[k], self.c, self.mate)

    def core_start(self, k, cols):
        self.s0[k] = self.part[1 - self.role, :, cols].astype(jnp.bfloat16)
        self.core_copy(k).start()

    def chip_start(self):
        for k in range(KVH):
            self.core_copy(k).wait_recv()
            cols = slice(k * D, (k + 1) * D)
            total = self.part[self.role, :, cols] + self.r0[k].astype(jnp.float32)
            self.acc[:, cols] = total
            self.s1[:, cols] = total.astype(jnp.bfloat16)
        self.copies = []
        for s in range(1, 16):
            ctx, resp, other = self.target(s)
            rows = self.s1.at[pl.ds(pl.multiple_of(other * 32, 32), 32)]
            self.copies.append(remote(rows, self.r1.at[s], self.ss.at[8 + s], self.rs.at[8 + s], ctx, resp))
        for copy in self.copies:
            copy.start()

    def z_copies(self):
        out = []
        for q in range(4):
            to = 4 * self.ylo + q
            for b, resp in enumerate((self.r, self.other_y)):
                copy = remote(
                    self.acc2.at[q],
                    self.r2.at[self.z],
                    self.zs.at[2 * q + b],
                    self.zr.at[self.z],
                    self.xy * NZ + to,
                    resp,
                )
                out.append((None if b else to != self.z, copy))
        return out

    def z_start(self):
        me = self.xy * 2 + self.ylo
        total = self.acc[pl.ds(pl.multiple_of(me * 32, 32), 32), :]
        for s, copy in enumerate(self.copies, 1):
            copy.wait_recv()
            total = total + self.r1[s].astype(jnp.float32)
        self.acc2[...] = total.reshape(4, 8, 512)
        for condition, copy in self.z_copies():
            Gather.when(condition, copy.start)

    def mate_start(self):
        z = self.z
        mine = z // 4 == self.ylo

        @pl.when(mine)
        def _():
            self.r2[z] = self.acc2[lax.rem(z, 4)]

        for i in range(NZ):

            @pl.when(jnp.logical_not(mine & (z == i)))
            def _(i=i):
                slot = self.r2.at[i]
                remote(slot, slot, self.zs.at[0], self.zr.at[i], self.c, self.r).wait_recv()

        total = self.r2[0]
        for i in range(1, NZ):
            total = total + self.r2[i]
        self.s3[...] = total
        self.last = remote(self.s3, self.r3, self.ss.at[8], self.rs.at[8], self.c, self.mate)
        self.last.start()

    def finish(self):
        self.last.wait_recv()
        mine, other = self.s3[...], self.r3[...]
        self.ko[...] = jnp.where(self.role == 0, mine, other).astype(jnp.bfloat16)
        self.vo[...] = jnp.where(self.role == 0, other, mine).astype(jnp.bfloat16)
        for copy in [self.core_copy(k) for k in range(KVH)] + self.copies + [self.last]:
            copy.wait_send()
        for condition, copy in self.z_copies():
            Gather.when(condition, copy.wait_send)


REDUCE_SCRATCH = [
    pltpu.VMEM((KVH, PR, D), jnp.bfloat16),
    pltpu.VMEM((KVH, PR, D), jnp.bfloat16),
    pltpu.VMEM((PR, 512), jnp.float32),
    pltpu.VMEM((PR, 512), jnp.bfloat16),
    pltpu.VMEM((16, 32, 512), jnp.bfloat16),
    pltpu.VMEM((4, 8, 512), jnp.float32),
    pltpu.VMEM((NZ, 8, 512), jnp.float32),
    pltpu.VMEM((8, 512), jnp.float32),
    pltpu.VMEM((8, 512), jnp.float32),
    pltpu.SemaphoreType.DMA((24,)),
    pltpu.SemaphoreType.DMA((24,)),
    pltpu.SemaphoreType.DMA((8,)),
    pltpu.SemaphoreType.DMA((8,)),
]


GATHER_SCRATCH = [
    pltpu.VMEM((2, 17, T, 512), jnp.bfloat16),
    pltpu.VMEM((2, PR, 512), jnp.bfloat16),
    pltpu.VMEM((NZ, 8, 512), jnp.float32),
    pltpu.SemaphoreType.DMA((6 * ROUNDS,)),
    pltpu.SemaphoreType.DMA((2 * OWN,)),
    pltpu.SemaphoreType.DMA((16,)),
    pltpu.SemaphoreType.DMA((16,)),
]
OWN_SCRATCH = [
    pltpu.VMEM((T, HQ * D), jnp.bfloat16),
    pltpu.VMEM((T, HQ * D), jnp.bfloat16),
    pltpu.VMEM((2, PR, 512), jnp.float32),
    pltpu.SemaphoreType.DMA((4,)),
]


def kernel(q_in, do_in, k_in, v_in, pk, pv, lengths, dq, ko, vo, *scratch):
    ng, no, na = len(GATHER_SCRATCH), len(OWN_SCRATCH), len(ATTEND_SCRATCH)
    gather_refs, own_refs = scratch[:ng], scratch[ng : ng + no]
    q, do, part, sems = own_refs
    g = Gather(*gather_refs)
    r = Reduce(part, ko, vo, scratch[ng + no + na :])
    a = Attend(q, do, g.kv, g.pg, lengths, scratch[ng + no : ng + no + na])
    loads = [
        pltpu.make_async_copy(k_in, g.kv.at[0, OWN], sems.at[0]),
        pltpu.make_async_copy(v_in, g.kv.at[1, OWN], sems.at[1]),
        pltpu.make_async_copy(q_in, q, sems.at[2]),
        pltpu.make_async_copy(do_in, do, sems.at[3]),
    ]
    for copy in loads:
        copy.start()
    barrier, arrivals = greet(r.peers())
    for copy in loads:
        copy.wait()
    a.prepare()
    pl.semaphore_wait(barrier, arrivals)
    g.prompt_z(pk, pv)
    words = g.tables()
    g.start_round(0, 0, words)
    g.start_round(1, 0, words)
    g.prompt_pair()
    a.slot_block(OWN)

    def one_round(t, words):
        later = g.following(words)
        for half in range(2):
            g.take_round(half, words)
            pl.when(t < ROUNDS)(lambda half=half: g.start_round(half, t, later))
        pl.when(t == 1)(lambda: g.prompt_hop(0))
        pl.when(t == 2)(lambda: g.prompt_hop(2))
        slots = g.received(words)

        @pl.loop(0, 3)
        def _(i):
            slot = jnp.where(i == 0, slots[0], jnp.where(i == 1, slots[1], slots[2]))
            pl.when(slot != NONE)(lambda: a.slot_block(slot))

        pl.when(t == 1)(lambda: g.prompt_hop(1))
        pl.when(t == 2)(lambda: g.prompt_hop(3))
        pl.when(t == 3)(g.prompt_done)
        low = jnp.minimum(jnp.maximum(t - 3, 0), 2) + 2 * (t // ROUNDS)
        high = jnp.maximum(t - 2, 0) + t // 5 - t // ROUNDS

        @pl.loop(0, 2)
        def _(i):
            pl.when(low + i < high)(lambda: a.prompt_block(low + i))

        return later

    lax.fori_loop(1, ROUNDS + 1, one_round, words)
    a.settle()
    a.prompt_grads(part, r.core_start)
    r.chip_start()
    a.prompt_dq()
    a.slot_grads(OWN)

    @pl.loop(0, 5)
    def _(pair):
        a.pair_grads(pair)

    r.z_start()

    @pl.loop(5, 8)
    def _(pair):
        a.pair_grads(pair)

    r.mate_start()
    a.store(dq)
    r.finish()
    g.prompt_sent()
    g.finish(words)


VM = pl.BlockSpec(memory_space=pltpu.VMEM)
SM = pl.BlockSpec(memory_space=pltpu.SMEM)
ANY = pl.BlockSpec(memory_space=pl.ANY)
MIB = 2**20


def body(queries, cotangent, sampled_keys, sampled_values, prompt_keys, prompt_values, lengths):
    dq, ko, vo = pl.pallas_call(
        kernel,
        out_shape=(
            jax.ShapeDtypeStruct((T, HQ * D), jnp.bfloat16),
            jax.ShapeDtypeStruct((8, 512), jnp.bfloat16),
            jax.ShapeDtypeStruct((8, 512), jnp.bfloat16),
        ),
        in_specs=[ANY] * 4 + [VM] * 2 + [SM],
        out_specs=(VM, VM, VM),
        scratch_shapes=GATHER_SCRATCH + OWN_SCRATCH + ATTEND_SCRATCH + REDUCE_SCRATCH,
        compiler_params=pltpu.CompilerParams(
            collective_id=0, has_side_effects=True, vmem_limit_bytes=62 * MIB
        ),
        name="shared_prompt_backward",
    )(queries[0], cotangent[0], sampled_keys[0], sampled_values[0], prompt_keys, prompt_values, lengths)
    return dq[None], ko, vo


def solution(mesh):
    rows = P("resp", "ctx", None)
    in_specs = (rows, rows, rows, rows, P("ctx", None), P("ctx", None), P("resp", None))
    out_specs = (rows, P("ctx", None), P("ctx", None))
    return jax.shard_map(body, mesh=mesh, in_specs=in_specs, out_specs=out_specs, check_vma=False)
```

```python
import jax
import jax.numpy as jnp
from jax import lax
from jax.experimental import pallas as pl
from jax.experimental.pallas import tpu as pltpu
from jax.sharding import PartitionSpec as P

D = 128
KVH = 4
QPK = 5
HQ = KVH * QPK
T = 128
PR = 512
G = QPK * T
NZ = 8
NXY = 8
ROUNDS = 6
NONE = 31
FROM_BELOW = (416751103, 216251648, 477602817, 1056210978, 508888131, 1050708068, 1041304709, 35754150)
FROM_ABOVE = (137734463, 181808479, 207008127, 273102239, 241187263, 510853599, 317956127, 1052058880)
FROM_BEFORE = (174130184, 1044482089, 1043472458, 241346667, 1048882316, 412363949, 380022990, 1053210863)
TO_ABOVE = (216251664, 477602832, 1056210992, 508888144, 1050708080, 1041304720, 35754160, 416751103)
TO_BELOW = (1052058896, 137734463, 181808479, 207008127, 273102239, 241187263, 510853599, 317956127)
SCALE = D ** (-0.5)
LOG2E = 1.4426950408889634
NEG = -1e30
OWN = 16
PROMPT = 17 * T
KEYS = 17 * T + PR
MESH = pl.DeviceIdType.MESH


def remote(src, dst, send, recv, ctx, resp):
    return pltpu.make_async_remote_copy(
        src_ref=src,
        dst_ref=dst,
        send_sem=send,
        recv_sem=recv,
        device_id=(ctx, resp),
        device_id_type=MESH,
    )


def place():
    c = lax.axis_index("ctx")
    r = lax.axis_index("resp")
    z = lax.rem(c, NZ)
    xy = c // NZ
    role = lax.rem(r, 2)
    return c, r, z, xy, role, r + 1 - 2 * role


def greet(peers):
    barrier = pltpu.get_barrier_semaphore()
    for ctx, resp in peers:
        pl.semaphore_signal(barrier, inc=1, device_id=(ctx, resp), device_id_type=MESH)
    return barrier, len(peers)


class Gather:
    def __init__(self, kv, pg, za, ks, kr, ps, pr):
        self.kv, self.pg, self.za = kv, pg, za
        self.ks, self.kr, self.ps, self.pr = ks, kr, ps, pr
        self.c, self.r, self.z, self.xy, self.role, self.mate = place()

    def peers(self):
        out = []
        for s in range(1, NZ):
            out.append((self.xy * NZ + lax.rem(self.z + s, NZ), self.r))
        for s in range(1, NXY):
            out.append((lax.rem(self.xy + s, NXY) * NZ + self.z, self.r))
        out.append((self.c, self.mate))
        return out

    def piece(self, half, src, dst, send, ctx):
        return remote(
            self.kv.at[half, src],
            self.kv.at[half, dst],
            self.ks.at[half * 3 * ROUNDS + send],
            self.kr.at[half * OWN + dst],
            ctx,
            self.r,
        )

    def arrived(self, half, slot):
        self.piece(half, slot, slot, 0, self.c).wait_recv()

    @staticmethod
    def when(condition, do):
        if condition is None:
            do()
        else:
            pl.when(condition)(do)

    def tables(self):
        def row(table):
            word = self.z * 0
            for i in range(NZ):
                word = word + (self.z == i).astype(jnp.int32) * table[i]
            return word

        return tuple(row(t) for t in (FROM_BELOW, FROM_ABOVE, FROM_BEFORE, TO_ABOVE, TO_BELOW))

    def sends(self, t, words):
        z = self.z
        t = z * 0 + t
        out = []
        for link, (word, by) in enumerate(((words[3], 1), (words[4], NZ - 1))):
            src = lax.rem(word, 32)
            dst = jnp.where(src == OWN, z, src)
            to = self.xy * NZ + lax.rem(z + by, NZ)
            out.append((src != NONE, (jnp.minimum(src, OWN), jnp.minimum(dst, OWN - 1), link * ROUNDS + t, to)))
        dst = lax.rem(words[2], 32)
        earlier = jnp.where(dst == NZ + z, OWN, jnp.where(dst < NZ, dst + NZ, dst - NZ))
        src = jnp.where(t == 1, OWN, earlier)
        to = lax.rem(self.c + NZ * (1 + (t == 1).astype(jnp.int32)), NZ * NXY)
        out.append((dst != NONE, (jnp.minimum(src, OWN), jnp.minimum(dst, OWN - 1), 2 * ROUNDS + t, to)))
        return out

    def start_round(self, half, t, words):
        for condition, what in self.sends(t, words):
            pl.when(condition)(lambda what=what: self.piece(half, *what).start())

    def received(self, words):
        return [lax.rem(word, 32) for word in words[:3]]

    def take_round(self, half, words):
        for slot in self.received(words):
            pl.when(slot != NONE)(lambda slot=slot: self.arrived(half, slot))

    @staticmethod
    def following(words):
        return tuple(word // 32 for word in words)

    def finish(self, words):
        def one(t, words):
            for condition, what in self.sends(t, words):
                for half in range(2):
                    pl.when(condition)(lambda half=half, what=what: self.piece(half, *what).wait_send())
            return self.following(words)

        lax.fori_loop(0, ROUNDS, one, words)

    def prompt_z(self, pk, pv):
        z = self.z
        mine = jnp.where(self.role == 0, pk[...].astype(jnp.float32), pv[...].astype(jnp.float32))
        self.za[z] = mine
        self.zcopies = [
            remote(
                self.za.at[z],
                self.za.at[z],
                self.ps.at[s],
                self.pr.at[s],
                self.xy * NZ + lax.rem(z + s, NZ),
                self.r,
            )
            for s in range(1, NZ)
        ]
        for copy in self.zcopies:
            copy.start()

    def prompt_pair(self):
        for s in range(1, NZ):
            source = lax.rem(self.z - s + NZ, NZ)
            remote(self.za.at[source], self.za.at[source], self.ps.at[s], self.pr.at[s], self.c, self.r).wait_recv()
        rows = pl.ds(pl.multiple_of(self.xy * 64, 64), 64)
        self.pg[self.role, rows, :] = self.za[...].reshape(64, 512).astype(jnp.bfloat16)
        self.pair_copy(self.xy).start()

    def pair_copy(self, xy):
        block = self.pg.at[self.role, pl.ds(pl.multiple_of(xy * 64, 64), 64)]
        to = self.xy + 1 - 2 * lax.rem(self.xy, 2)
        return remote(block, block, self.ps.at[8], self.pr.at[8], to * NZ + self.z, self.r)

    def x_copy(self, k):
        x = lax.rem(self.xy // 2 + k, 4)
        block = self.pg.at[self.role, pl.ds(pl.multiple_of(x * 128, 128), 128)]
        to = lax.rem(self.c + 6 * NZ, NXY * NZ)
        return remote(block, block, self.ps.at[9 + k], self.pr.at[9 + k], to, self.r)

    def prompt_hop(self, k):
        if k == 0:
            self.pair_copy(self.xy + 1 - 2 * lax.rem(self.xy, 2)).wait_recv()
        else:
            x = lax.rem(self.xy // 2 + k, 4)
            block = self.pg.at[self.role, pl.ds(pl.multiple_of(x * 128, 128), 128)]
            remote(block, block, self.ps.at[8 + k], self.pr.at[8 + k], self.c, self.r).wait_recv()
        if k < 3:
            self.x_copy(k).start()
        else:
            self.core_copy().start()

    def core_copy(self):
        half = self.pg.at[self.role]
        return remote(half, half, self.ps.at[0], self.pr.at[0], self.c, self.mate)

    def prompt_done(self):
        other = self.pg.at[1 - self.role]
        remote(other, other, self.ps.at[0], self.pr.at[0], self.c, self.mate).wait_recv()

    def prompt_sent(self):
        for copy in self.zcopies + [self.pair_copy(self.xy)] + [self.x_copy(k) for k in range(3)] + [self.core_copy()]:
            copy.wait_send()


class Attend:
    def __init__(self, q, do, kv, pg, lengths, sc):
        self.q, self.do, self.kv, self.pg, self.lengths = q, do, kv, pg, lengths
        (self.qt, self.dot_, self.qn, self.don, self.e, self.ep, self.dp) = sc[:7]
        (self.m, self.l, self.w, self.mb, self.dq) = sc[7:]

    def prepare(self):
        for k in range(KVH):
            for h in range(QPK):
                cols = slice((k * QPK + h) * D, (k * QPK + h + 1) * D)
                rows = slice(h * T, (h + 1) * T)
                self.qn[k, rows, :] = self.q[:, cols]
                self.don[k, rows, :] = self.do[:, cols]
                self.qt[k, :, rows] = self.q[:, cols].T
                self.dot_[k, :, rows] = self.do[:, cols].T
        self.m[...] = jnp.full(self.m.shape, NEG, jnp.float32)
        self.l[...] = jnp.zeros(self.l.shape, jnp.float32)
        self.w[...] = jnp.zeros(self.w.shape, jnp.float32)
        self.dq[...] = jnp.zeros(self.dq.shape, jnp.float32)
        c = lax.axis_index("ctx")
        self.first = c * T
        self.qpos = self.first + lax.broadcasted_iota(jnp.int32, (1, T), 1)
        start = jnp.zeros((1, T), jnp.int32)
        end = jnp.int32(0)
        for s in range(8):
            end = end + self.lengths[0, s]
            start = jnp.where(self.qpos >= end, end, start)
        self.start = start

    def bias(self, slot):
        c = lax.axis_index("ctx")
        z = lax.rem(c, NZ)
        if isinstance(slot, int) and slot == OWN:
            base = c
        else:
            part = lax.rem(slot, NZ)
            near = c - z + part
            base = jnp.where(slot < NZ, jnp.where(part < z, near, near - 2 * NZ), near - NZ)
        pos = base * T + lax.broadcasted_iota(jnp.int32, (T, T), 0)
        visible = (pos >= self.start) & (pos <= self.qpos)
        return jnp.where(visible, 0.0, NEG).astype(jnp.float32)

    def forward(self, keys, values, bias, row, block, n):
        @pl.loop(0, KVH, unroll=True)
        def _(k):
            s = jnp.dot(keys(k), self.qt[k], preferred_element_type=jnp.float32)
            dp = jnp.dot(values(k), self.dot_[k], preferred_element_type=jnp.float32)
            self.dp[k, pl.ds(row, n), :] = dp
            for h in range(QPK):
                cols = slice(h * T, (h + 1) * T)
                x = s[:, cols] * (SCALE * LOG2E)
                if bias is not None:
                    x = x + bias
                old = self.m[k, :, cols]
                new = jnp.maximum(old, jnp.max(x, axis=0, keepdims=True))
                f = jnp.exp2(old - new)
                e = jnp.exp2(x - new)
                self.m[k, :, cols] = new
                self.mb[block, k, :, cols] = new
                self.l[k, :, cols] = self.l[k, :, cols] * f + jnp.sum(e, axis=0, keepdims=True)
                self.w[k, :, cols] = self.w[k, :, cols] * f + jnp.sum(e * dp[:, cols], axis=0, keepdims=True)
                if bias is None:
                    self.ep[k, pl.ds(row - PROMPT, n), cols] = e
                else:
                    self.e[k, pl.ds(row, n), cols] = e.astype(jnp.bfloat16)

    def slot_block(self, slot):
        bias = self.bias(slot)
        row = slot * T if isinstance(slot, int) else pl.multiple_of(slot * T, T)
        self.forward(
            lambda k: self.kv[0, slot, :, pl.ds(pl.multiple_of(k * D, D), D)],
            lambda k: self.kv[1, slot, :, pl.ds(pl.multiple_of(k * D, D), D)],
            bias,
            row,
            slot,
            T,
        )

    def prompt_block(self, i):
        rows = pl.ds(pl.multiple_of(i * T, T), T)
        self.forward(
            lambda k: self.pg[0, rows, pl.ds(pl.multiple_of(k * D, D), D)],
            lambda k: self.pg[1, rows, pl.ds(pl.multiple_of(k * D, D), D)],
            None,
            pl.multiple_of(PROMPT + i * T, T),
            17 + i,
            T,
        )

    def settle(self):
        self.l[...] = 1.0 / self.l[...]
        self.w[...] = self.w[...] * self.l[...]

    def grads(self, k, block, row, e):
        f = jnp.exp2(self.mb[block, k] - self.m[k]) * self.l[k]
        p = e * f
        ds = (p * ((self.dp[k, pl.ds(row, T), :] - self.w[k]) * SCALE)).astype(jnp.bfloat16)
        return p, ds

    def slot_e(self, k, row):
        return self.e[k, pl.ds(row, T), :].astype(jnp.float32)

    def add_dq(self, k, keys, ds):
        self.dq[k] += lax.dot_general(keys, ds, (((0,), (0,)), ((), ())), preferred_element_type=jnp.float32)

    def prompt_grads(self, part, ready):
        @pl.loop(0, KVH)
        def _(k):
            cols = pl.ds(pl.multiple_of(k * D, D), D)
            for i in range(4):
                rows = slice(i * T, (i + 1) * T)
                p, ds = self.grads(k, 17 + i, PROMPT + i * T, self.ep[k, rows, :])
                self.ep[k, rows, :] = ds.astype(jnp.float32)
                part[0, rows, cols] = jnp.dot(ds, self.qn[k], preferred_element_type=jnp.float32)
                part[1, rows, cols] = jnp.dot(p.astype(jnp.bfloat16), self.don[k], preferred_element_type=jnp.float32)
            ready(k, cols)

    def prompt_dq(self):
        @pl.loop(0, KVH)
        def _(k):
            cols = pl.ds(pl.multiple_of(k * D, D), D)
            self.add_dq(k, self.pg[0, :, cols], self.ep[k].astype(jnp.bfloat16))

    def slot_grads(self, slot):
        row = slot * T if isinstance(slot, int) else pl.multiple_of(slot * T, T)

        @pl.loop(0, KVH)
        def _(k):
            _, ds = self.grads(k, slot, row, self.slot_e(k, row))
            self.add_dq(k, self.kv[0, slot, :, pl.ds(pl.multiple_of(k * D, D), D)], ds)

    def pair_grads(self, pair):
        row = pl.multiple_of(pair * 2 * T, 2 * T)

        @pl.loop(0, KVH)
        def _(k):
            _, d0 = self.grads(k, 2 * pair, row, self.slot_e(k, row))
            _, d1 = self.grads(k, 2 * pair + 1, row + T, self.slot_e(k, row + T))
            cols = pl.ds(pl.multiple_of(k * D, D), D)
            keys = self.kv[0, pl.ds(2 * pair, 2), :, cols].reshape(2 * T, D)
            self.add_dq(k, keys, jnp.concatenate([d0, d1], axis=0))

    def store(self, out):
        for k in range(KVH):
            for h in range(QPK):
                hd = k * QPK + h
                out[:, hd * D : (hd + 1) * D] = self.dq[k, :, h * T : (h + 1) * T].T.astype(jnp.bfloat16)


ATTEND_SCRATCH = [
    pltpu.VMEM((KVH, D, G), jnp.bfloat16),
    pltpu.VMEM((KVH, D, G), jnp.bfloat16),
    pltpu.VMEM((KVH, G, D), jnp.bfloat16),
    pltpu.VMEM((KVH, G, D), jnp.bfloat16),
    pltpu.VMEM((KVH, 17 * T, G), jnp.bfloat16),
    pltpu.VMEM((KVH, PR, G), jnp.float32),
    pltpu.VMEM((KVH, KEYS, G), jnp.float32),
    pltpu.VMEM((KVH, 1, G), jnp.float32),
    pltpu.VMEM((KVH, 1, G), jnp.float32),
    pltpu.VMEM((KVH, 1, G), jnp.float32),
    pltpu.VMEM((21, KVH, 1, G), jnp.float32),
    pltpu.VMEM((KVH, D, G), jnp.float32),
]


class Reduce:
    def __init__(self, part, ko, vo, sc):
        self.part, self.ko, self.vo = part, ko, vo
        (self.s0, self.r0, self.acc, self.s1, self.r1, self.acc2, self.r2, self.res) = sc[:8]
        self.ss, self.rs, self.zs, self.zr = sc[8:]
        self.c, self.r, self.z, self.xy, self.role, self.mate = place()
        self.ylo = self.r // 2
        self.other_y = (1 - self.ylo) * 2 + self.role
        self.far = (1 - self.ylo) * 2 + 1 - self.role

    def peers(self):
        out = [(self.c, self.mate), (self.c, self.far)]
        for s in range(1, NZ):
            out.append((self.xy * NZ + lax.rem(self.z + s, NZ), self.r))
        for s in range(1, 16):
            out.append(self.target(s)[:2])
        return out

    def target(self, s):
        me = self.xy * 2 + self.ylo
        other = lax.rem(me + s, 16)
        return (other // 2) * NZ + self.z, lax.rem(other, 2) * 2 + self.role, other

    def core_copy(self, k):
        return remote(self.s0.at[k], self.r0.at[k], self.ss.at[k], self.rs.at[k], self.c, self.mate)

    def core_start(self, k, cols):
        self.s0[k] = self.part[1 - self.role, :, cols].astype(jnp.bfloat16)
        self.core_copy(k).start()

    def chip_start(self):
        for k in range(KVH):
            self.core_copy(k).wait_recv()
            cols = slice(k * D, (k + 1) * D)
            total = self.part[self.role, :, cols] + self.r0[k].astype(jnp.float32)
            self.acc[:, cols] = total
            self.s1[:, cols] = total.astype(jnp.bfloat16)
        self.copies = []
        for s in range(1, 16):
            ctx, resp, other = self.target(s)
            rows = self.s1.at[pl.ds(pl.multiple_of(other * 32, 32), 32)]
            self.copies.append(remote(rows, self.r1.at[s], self.ss.at[8 + s], self.rs.at[8 + s], ctx, resp))
        for copy in self.copies:
            copy.start()

    def z_copies(self):
        out = []
        for q in range(4):
            to = 4 * self.ylo + q
            copy = remote(
                self.acc2.at[q], self.r2.at[self.z], self.zs.at[q], self.zr.at[self.z], self.xy * NZ + to, self.r
            )
            out.append((to != self.z, copy))
        return out

    def z_start(self):
        me = self.xy * 2 + self.ylo
        total = self.acc[pl.ds(pl.multiple_of(me * 32, 32), 32), :]
        for s, copy in enumerate(self.copies, 1):
            copy.wait_recv()
            total = total + self.r1[s].astype(jnp.float32)
        self.acc2[...] = total.reshape(4, 8, 512)
        for condition, copy in self.z_copies():
            Gather.when(condition, copy.start)

    def out_copies(self):
        block = self.res.at[self.role]
        places = (self.mate, self.other_y, self.far)
        return [
            remote(block, block, self.zs.at[4 + i], self.rs.at[4 + self.role], self.c, resp)
            for i, resp in enumerate(places)
        ]

    def owners_start(self):
        z = self.z

        @pl.when(z // 4 == self.ylo)
        def _():
            self.r2[z] = self.acc2[lax.rem(z, 4)]
            for i in range(NZ):

                @pl.when(z != i)
                def _(i=i):
                    slot = self.r2.at[i]
                    remote(slot, slot, self.zs.at[0], self.zr.at[i], self.c, self.r).wait_recv()

            total = self.r2[0]
            for i in range(1, NZ):
                total = total + self.r2[i]
            self.res[self.role] = total
            for copy in self.out_copies():
                copy.start()

    def finish(self):
        owner = self.z // 4 == self.ylo
        for i in range(2):

            @pl.when(jnp.logical_not(owner & (self.role == i)))
            def _(i=i):
                block = self.res.at[i]
                remote(block, block, self.zs.at[0], self.rs.at[4 + i], self.c, self.mate).wait_recv()

        self.ko[...] = self.res[0].astype(jnp.bfloat16)
        self.vo[...] = self.res[1].astype(jnp.bfloat16)
        for copy in [self.core_copy(k) for k in range(KVH)] + self.copies:
            copy.wait_send()
        for condition, copy in self.z_copies():
            Gather.when(condition, copy.wait_send)

        @pl.when(owner)
        def _():
            for copy in self.out_copies():
                copy.wait_send()


REDUCE_SCRATCH = [
    pltpu.VMEM((KVH, PR, D), jnp.bfloat16),
    pltpu.VMEM((KVH, PR, D), jnp.bfloat16),
    pltpu.VMEM((PR, 512), jnp.float32),
    pltpu.VMEM((PR, 512), jnp.bfloat16),
    pltpu.VMEM((16, 32, 512), jnp.bfloat16),
    pltpu.VMEM((4, 8, 512), jnp.float32),
    pltpu.VMEM((NZ, 8, 512), jnp.float32),
    pltpu.VMEM((2, 8, 512), jnp.float32),
    pltpu.SemaphoreType.DMA((24,)),
    pltpu.SemaphoreType.DMA((24,)),
    pltpu.SemaphoreType.DMA((8,)),
    pltpu.SemaphoreType.DMA((8,)),
]


GATHER_SCRATCH = [
    pltpu.VMEM((2, 17, T, 512), jnp.bfloat16),
    pltpu.VMEM((2, PR, 512), jnp.bfloat16),
    pltpu.VMEM((NZ, 8, 512), jnp.float32),
    pltpu.SemaphoreType.DMA((6 * ROUNDS,)),
    pltpu.SemaphoreType.DMA((2 * OWN,)),
    pltpu.SemaphoreType.DMA((16,)),
    pltpu.SemaphoreType.DMA((16,)),
]
OWN_SCRATCH = [
    pltpu.VMEM((T, HQ * D), jnp.bfloat16),
    pltpu.VMEM((T, HQ * D), jnp.bfloat16),
    pltpu.VMEM((2, PR, 512), jnp.float32),
    pltpu.SemaphoreType.DMA((4,)),
]


def kernel(q_in, do_in, k_in, v_in, pk, pv, lengths, dq, ko, vo, *scratch):
    ng, no, na = len(GATHER_SCRATCH), len(OWN_SCRATCH), len(ATTEND_SCRATCH)
    gather_refs, own_refs = scratch[:ng], scratch[ng : ng + no]
    q, do, part, sems = own_refs
    g = Gather(*gather_refs)
    r = Reduce(part, ko, vo, scratch[ng + no + na :])
    a = Attend(q, do, g.kv, g.pg, lengths, scratch[ng + no : ng + no + na])
    loads = [
        pltpu.make_async_copy(k_in, g.kv.at[0, OWN], sems.at[0]),
        pltpu.make_async_copy(v_in, g.kv.at[1, OWN], sems.at[1]),
        pltpu.make_async_copy(q_in, q, sems.at[2]),
        pltpu.make_async_copy(do_in, do, sems.at[3]),
    ]
    for copy in loads:
        copy.start()
    barrier, arrivals = greet(r.peers())
    for copy in loads:
        copy.wait()
    a.prepare()
    pl.semaphore_wait(barrier, arrivals)
    g.prompt_z(pk, pv)
    words = g.tables()
    g.start_round(0, 0, words)
    g.start_round(1, 0, words)
    g.prompt_pair()
    a.slot_block(OWN)

    def one_round(t, words):
        later = g.following(words)
        for half in range(2):
            g.take_round(half, words)
            pl.when(t < ROUNDS)(lambda half=half: g.start_round(half, t, later))
        pl.when(t == 1)(lambda: g.prompt_hop(0))
        pl.when(t == 3)(lambda: g.prompt_hop(3))
        slots = g.received(words)

        @pl.loop(0, 3)
        def _(i):
            slot = jnp.where(i == 0, slots[0], jnp.where(i == 1, slots[1], slots[2]))
            pl.when(slot != NONE)(lambda: a.slot_block(slot))

        pl.when(t == 1)(lambda: g.prompt_hop(1))
        pl.when(t == 2)(lambda: g.prompt_hop(2))
        pl.when(t == 3)(g.prompt_done)
        low = 1 * (t > 3).astype(jnp.int32) + 2 * (t > 4).astype(jnp.int32) + 1 * (t > 5).astype(jnp.int32)
        high = 1 * (t >= 3).astype(jnp.int32) + 2 * (t >= 4).astype(jnp.int32) + 1 * (t >= 5).astype(jnp.int32)

        @pl.loop(0, 2)
        def _(i):
            pl.when(low + i < high)(lambda: a.prompt_block(low + i))

        return later

    lax.fori_loop(1, ROUNDS + 1, one_round, words)
    a.settle()
    a.prompt_grads(part, r.core_start)
    r.chip_start()
    a.prompt_dq()
    a.slot_grads(OWN)

    @pl.loop(0, 5)
    def _(pair):
        a.pair_grads(pair)

    r.z_start()

    @pl.loop(5, 8)
    def _(pair):
        a.pair_grads(pair)

    r.owners_start()
    a.store(dq)
    r.finish()
    g.prompt_sent()
    g.finish(words)


VM = pl.BlockSpec(memory_space=pltpu.VMEM)
SM = pl.BlockSpec(memory_space=pltpu.SMEM)
ANY = pl.BlockSpec(memory_space=pl.ANY)
MIB = 2**20


def body(queries, cotangent, sampled_keys, sampled_values, prompt_keys, prompt_values, lengths):
    dq, ko, vo = pl.pallas_call(
        kernel,
        out_shape=(
            jax.ShapeDtypeStruct((T, HQ * D), jnp.bfloat16),
            jax.ShapeDtypeStruct((8, 512), jnp.bfloat16),
            jax.ShapeDtypeStruct((8, 512), jnp.bfloat16),
        ),
        in_specs=[ANY] * 4 + [VM] * 2 + [SM],
        out_specs=(VM, VM, VM),
        scratch_shapes=GATHER_SCRATCH + OWN_SCRATCH + ATTEND_SCRATCH + REDUCE_SCRATCH,
        compiler_params=pltpu.CompilerParams(
            collective_id=0, has_side_effects=True, vmem_limit_bytes=62 * MIB
        ),
        name="shared_prompt_backward",
    )(queries[0], cotangent[0], sampled_keys[0], sampled_values[0], prompt_keys, prompt_values, lengths)
    return dq[None], ko, vo


def solution(mesh):
    rows = P("resp", "ctx", None)
    in_specs = (rows, rows, rows, rows, P("ctx", None), P("ctx", None), P("resp", None))
    out_specs = (rows, P("ctx", None), P("ctx", None))
    return jax.shard_map(body, mesh=mesh, in_specs=in_specs, out_specs=out_specs, check_vma=False)
```

```python
import jax
import jax.numpy as jnp
from jax import lax
from jax.experimental import pallas as pl
from jax.experimental.pallas import tpu as pltpu
from jax.sharding import PartitionSpec as P

D = 128
KVH = 4
QPK = 5
HQ = KVH * QPK
T = 128
PR = 512
G = QPK * T
NZ = 8
NXY = 8
ROUNDS = 6
NONE = 31
FROM_BELOW = (416751103, 216251648, 477602817, 1056210978, 508888131, 1050708068, 1041304709, 35754150)
FROM_ABOVE = (137734463, 181808479, 207008127, 273102239, 241187263, 510853599, 317956127, 1052058880)
FROM_BEFORE = (174130184, 1044482089, 1043472458, 241346667, 1048882316, 412363949, 380022990, 1053210863)
TO_ABOVE = (216251664, 477602832, 1056210992, 508888144, 1050708080, 1041304720, 35754160, 416751103)
TO_BELOW = (1052058896, 137734463, 181808479, 207008127, 273102239, 241187263, 510853599, 317956127)
SCALE = D ** (-0.5)
LOG2E = 1.4426950408889634
NEG = -1e30
OWN = 16
PROMPT = 17 * T
KEYS = 17 * T + PR
MESH = pl.DeviceIdType.MESH


def remote(src, dst, send, recv, ctx, resp):
    return pltpu.make_async_remote_copy(
        src_ref=src,
        dst_ref=dst,
        send_sem=send,
        recv_sem=recv,
        device_id=(ctx, resp),
        device_id_type=MESH,
    )


def place():
    c = lax.axis_index("ctx")
    r = lax.axis_index("resp")
    z = lax.rem(c, NZ)
    xy = c // NZ
    role = lax.rem(r, 2)
    return c, r, z, xy, role, r + 1 - 2 * role


def greet(peers):
    barrier = pltpu.get_barrier_semaphore()
    for ctx, resp in peers:
        pl.semaphore_signal(barrier, inc=1, device_id=(ctx, resp), device_id_type=MESH)
    return barrier, len(peers)


class Gather:
    def __init__(self, kv, pg, za, ks, kr, ps, pr):
        self.kv, self.pg, self.za = kv, pg, za
        self.ks, self.kr, self.ps, self.pr = ks, kr, ps, pr
        self.c, self.r, self.z, self.xy, self.role, self.mate = place()

    def peers(self):
        out = []
        for s in range(1, NZ):
            out.append((self.xy * NZ + lax.rem(self.z + s, NZ), self.r))
        for s in range(1, NXY):
            out.append((lax.rem(self.xy + s, NXY) * NZ + self.z, self.r))
        out.append((self.c, self.mate))
        return out

    def piece(self, half, src, dst, send, ctx):
        return remote(
            self.kv.at[half, src],
            self.kv.at[half, dst],
            self.ks.at[half * 3 * ROUNDS + send],
            self.kr.at[half * OWN + dst],
            ctx,
            self.r,
        )

    def arrived(self, half, slot):
        self.piece(half, slot, slot, 0, self.c).wait_recv()

    @staticmethod
    def when(condition, do):
        if condition is None:
            do()
        else:
            pl.when(condition)(do)

    def tables(self):
        def row(table):
            word = self.z * 0
            for i in range(NZ):
                word = word + (self.z == i).astype(jnp.int32) * table[i]
            return word

        return tuple(row(t) for t in (FROM_BELOW, FROM_ABOVE, FROM_BEFORE, TO_ABOVE, TO_BELOW))

    def sends(self, t, words):
        z = self.z
        t = z * 0 + t
        out = []
        for link, (word, by) in enumerate(((words[3], 1), (words[4], NZ - 1))):
            src = lax.rem(word, 32)
            dst = jnp.where(src == OWN, z, src)
            to = self.xy * NZ + lax.rem(z + by, NZ)
            out.append((src != NONE, (jnp.minimum(src, OWN), jnp.minimum(dst, OWN - 1), link * ROUNDS + t, to)))
        dst = lax.rem(words[2], 32)
        earlier = jnp.where(dst == NZ + z, OWN, jnp.where(dst < NZ, dst + NZ, dst - NZ))
        src = jnp.where(t == 1, OWN, earlier)
        to = lax.rem(self.c + NZ * (1 + (t == 1).astype(jnp.int32)), NZ * NXY)
        out.append((dst != NONE, (jnp.minimum(src, OWN), jnp.minimum(dst, OWN - 1), 2 * ROUNDS + t, to)))
        return out

    def start_round(self, half, t, words):
        for condition, what in self.sends(t, words):
            pl.when(condition)(lambda what=what: self.piece(half, *what).start())

    def received(self, words):
        return [lax.rem(word, 32) for word in words[:3]]

    def take_round(self, half, words):
        for slot in self.received(words):
            pl.when(slot != NONE)(lambda slot=slot: self.arrived(half, slot))

    @staticmethod
    def following(words):
        return tuple(word // 32 for word in words)

    def finish(self, words):
        def one(t, words):
            for condition, what in self.sends(t, words):
                for half in range(2):
                    pl.when(condition)(lambda half=half, what=what: self.piece(half, *what).wait_send())
            return self.following(words)

        lax.fori_loop(0, ROUNDS, one, words)

    def prompt_z(self, pk, pv):
        z = self.z
        mine = jnp.where(self.role == 0, pk[...].astype(jnp.float32), pv[...].astype(jnp.float32))
        self.za[z] = mine
        self.zcopies = [
            remote(
                self.za.at[z],
                self.za.at[z],
                self.ps.at[s],
                self.pr.at[s],
                self.xy * NZ + lax.rem(z + s, NZ),
                self.r,
            )
            for s in range(1, NZ)
        ]
        for copy in self.zcopies:
            copy.start()

    def prompt_pair(self):
        for s in range(1, NZ):
            source = lax.rem(self.z - s + NZ, NZ)
            remote(self.za.at[source], self.za.at[source], self.ps.at[s], self.pr.at[s], self.c, self.r).wait_recv()
        rows = pl.ds(pl.multiple_of(self.xy * 64, 64), 64)
        self.pg[self.role, rows, :] = self.za[...].reshape(64, 512).astype(jnp.bfloat16)
        self.pair_copy(self.xy).start()

    def pair_copy(self, xy):
        block = self.pg.at[self.role, pl.ds(pl.multiple_of(xy * 64, 64), 64)]
        to = self.xy + 1 - 2 * lax.rem(self.xy, 2)
        return remote(block, block, self.ps.at[8], self.pr.at[8], to * NZ + self.z, self.r)

    def x_copy(self, k):
        x = lax.rem(self.xy // 2 + k, 4)
        block = self.pg.at[self.role, pl.ds(pl.multiple_of(x * 128, 128), 128)]
        to = lax.rem(self.c + 6 * NZ, NXY * NZ)
        return remote(block, block, self.ps.at[9 + k], self.pr.at[9 + k], to, self.r)

    def prompt_hop(self, k):
        if k == 0:
            self.pair_copy(self.xy + 1 - 2 * lax.rem(self.xy, 2)).wait_recv()
        else:
            x = lax.rem(self.xy // 2 + k, 4)
            block = self.pg.at[self.role, pl.ds(pl.multiple_of(x * 128, 128), 128)]
            remote(block, block, self.ps.at[8 + k], self.pr.at[8 + k], self.c, self.r).wait_recv()
        if k < 3:
            self.x_copy(k).start()
        else:
            self.core_copy().start()

    def core_copy(self):
        half = self.pg.at[self.role]
        return remote(half, half, self.ps.at[0], self.pr.at[0], self.c, self.mate)

    def prompt_done(self):
        other = self.pg.at[1 - self.role]
        remote(other, other, self.ps.at[0], self.pr.at[0], self.c, self.mate).wait_recv()

    def prompt_sent(self):
        for copy in self.zcopies + [self.pair_copy(self.xy)] + [self.x_copy(k) for k in range(3)] + [self.core_copy()]:
            copy.wait_send()


class Attend:
    def __init__(self, q, do, kv, pg, lengths, sc):
        self.q, self.do, self.kv, self.pg, self.lengths = q, do, kv, pg, lengths
        (self.qt, self.dot_, self.qn, self.don, self.e, self.ep, self.dp) = sc[:7]
        (self.m, self.l, self.w, self.mb, self.dq) = sc[7:]

    def prepare(self):
        for k in range(KVH):
            for h in range(QPK):
                cols = slice((k * QPK + h) * D, (k * QPK + h + 1) * D)
                rows = slice(h * T, (h + 1) * T)
                self.qn[k, rows, :] = self.q[:, cols]
                self.don[k, rows, :] = self.do[:, cols]
                self.qt[k, :, rows] = self.q[:, cols].T
                self.dot_[k, :, rows] = self.do[:, cols].T
        self.m[...] = jnp.full(self.m.shape, NEG, jnp.float32)
        self.l[...] = jnp.zeros(self.l.shape, jnp.float32)
        self.w[...] = jnp.zeros(self.w.shape, jnp.float32)
        self.dq[...] = jnp.zeros(self.dq.shape, jnp.float32)
        c = lax.axis_index("ctx")
        self.first = c * T
        self.qpos = self.first + lax.broadcasted_iota(jnp.int32, (1, T), 1)
        start = jnp.zeros((1, T), jnp.int32)
        end = jnp.int32(0)
        for s in range(8):
            end = end + self.lengths[0, s]
            start = jnp.where(self.qpos >= end, end, start)
        self.start = start

    def bias(self, slot):
        c = lax.axis_index("ctx")
        z = lax.rem(c, NZ)
        if isinstance(slot, int) and slot == OWN:
            base = c
        else:
            part = lax.rem(slot, NZ)
            near = c - z + part
            base = jnp.where(slot < NZ, jnp.where(part < z, near, near - 2 * NZ), near - NZ)
        pos = base * T + lax.broadcasted_iota(jnp.int32, (T, T), 0)
        visible = (pos >= self.start) & (pos <= self.qpos)
        return jnp.where(visible, 0.0, NEG).astype(jnp.float32)

    def forward(self, keys, values, bias, row, block, n):
        @pl.loop(0, KVH, unroll=True)
        def _(k):
            s = jnp.dot(keys(k), self.qt[k], preferred_element_type=jnp.float32)
            dp = jnp.dot(values(k), self.dot_[k], preferred_element_type=jnp.float32)
            self.dp[k, pl.ds(row, n), :] = dp
            for h in range(QPK):
                cols = slice(h * T, (h + 1) * T)
                x = s[:, cols] * (SCALE * LOG2E)
                if bias is not None:
                    x = x + bias
                old = self.m[k, :, cols]
                new = jnp.maximum(old, jnp.max(x, axis=0, keepdims=True))
                f = jnp.exp2(old - new)
                e = jnp.exp2(x - new)
                self.m[k, :, cols] = new
                self.mb[block, k, :, cols] = new
                self.l[k, :, cols] = self.l[k, :, cols] * f + jnp.sum(e, axis=0, keepdims=True)
                self.w[k, :, cols] = self.w[k, :, cols] * f + jnp.sum(e * dp[:, cols], axis=0, keepdims=True)
                if bias is None:
                    self.ep[k, pl.ds(row - PROMPT, n), cols] = e
                else:
                    self.e[k, pl.ds(row, n), cols] = e.astype(jnp.bfloat16)

    def slot_block(self, slot):
        bias = self.bias(slot)
        row = slot * T if isinstance(slot, int) else pl.multiple_of(slot * T, T)
        self.forward(
            lambda k: self.kv[0, slot, :, pl.ds(pl.multiple_of(k * D, D), D)],
            lambda k: self.kv[1, slot, :, pl.ds(pl.multiple_of(k * D, D), D)],
            bias,
            row,
            slot,
            T,
        )

    def prompt_block(self, i):
        rows = pl.ds(pl.multiple_of(i * T, T), T)
        self.forward(
            lambda k: self.pg[0, rows, pl.ds(pl.multiple_of(k * D, D), D)],
            lambda k: self.pg[1, rows, pl.ds(pl.multiple_of(k * D, D), D)],
            None,
            pl.multiple_of(PROMPT + i * T, T),
            17 + i,
            T,
        )

    def settle(self):
        self.l[...] = 1.0 / self.l[...]
        self.w[...] = self.w[...] * self.l[...]

    def grads(self, k, block, row, e):
        f = jnp.exp2(self.mb[block, k] - self.m[k]) * self.l[k]
        p = e * f
        ds = (p * ((self.dp[k, pl.ds(row, T), :] - self.w[k]) * SCALE)).astype(jnp.bfloat16)
        return p, ds

    def slot_e(self, k, row):
        return self.e[k, pl.ds(row, T), :].astype(jnp.float32)

    def add_dq(self, k, keys, ds):
        self.dq[k] += lax.dot_general(keys, ds, (((0,), (0,)), ((), ())), preferred_element_type=jnp.float32)

    def prompt_grads(self, part, ready):
        @pl.loop(0, KVH, unroll=True)
        def _(k):
            cols = pl.ds(pl.multiple_of(k * D, D), D)
            for i in range(4):
                rows = slice(i * T, (i + 1) * T)
                p, ds = self.grads(k, 17 + i, PROMPT + i * T, self.ep[k, rows, :])
                self.ep[k, rows, :] = ds.astype(jnp.float32)
                part[0, rows, cols] = jnp.dot(ds, self.qn[k], preferred_element_type=jnp.float32)
                part[1, rows, cols] = jnp.dot(p.astype(jnp.bfloat16), self.don[k], preferred_element_type=jnp.float32)
            ready(k, cols)

    def prompt_dq(self):
        @pl.loop(0, KVH)
        def _(k):
            cols = pl.ds(pl.multiple_of(k * D, D), D)
            self.add_dq(k, self.pg[0, :, cols], self.ep[k].astype(jnp.bfloat16))

    def slot_grads(self, slot):
        row = slot * T if isinstance(slot, int) else pl.multiple_of(slot * T, T)

        @pl.loop(0, KVH)
        def _(k):
            _, ds = self.grads(k, slot, row, self.slot_e(k, row))
            self.add_dq(k, self.kv[0, slot, :, pl.ds(pl.multiple_of(k * D, D), D)], ds)

    def pair_grads(self, pair):
        row = pl.multiple_of(pair * 2 * T, 2 * T)

        @pl.loop(0, KVH)
        def _(k):
            _, d0 = self.grads(k, 2 * pair, row, self.slot_e(k, row))
            _, d1 = self.grads(k, 2 * pair + 1, row + T, self.slot_e(k, row + T))
            cols = pl.ds(pl.multiple_of(k * D, D), D)
            keys = self.kv[0, pl.ds(2 * pair, 2), :, cols].reshape(2 * T, D)
            self.add_dq(k, keys, jnp.concatenate([d0, d1], axis=0))

    def store(self, out):
        for k in range(KVH):
            for h in range(QPK):
                hd = k * QPK + h
                out[:, hd * D : (hd + 1) * D] = self.dq[k, :, h * T : (h + 1) * T].T.astype(jnp.bfloat16)


ATTEND_SCRATCH = [
    pltpu.VMEM((KVH, D, G), jnp.bfloat16),
    pltpu.VMEM((KVH, D, G), jnp.bfloat16),
    pltpu.VMEM((KVH, G, D), jnp.bfloat16),
    pltpu.VMEM((KVH, G, D), jnp.bfloat16),
    pltpu.VMEM((KVH, 17 * T, G), jnp.bfloat16),
    pltpu.VMEM((KVH, PR, G), jnp.float32),
    pltpu.VMEM((KVH, KEYS, G), jnp.float32),
    pltpu.VMEM((KVH, 1, G), jnp.float32),
    pltpu.VMEM((KVH, 1, G), jnp.float32),
    pltpu.VMEM((KVH, 1, G), jnp.float32),
    pltpu.VMEM((21, KVH, 1, G), jnp.float32),
    pltpu.VMEM((KVH, D, G), jnp.float32),
]


class Reduce:
    def __init__(self, part, ko, vo, sc):
        self.part, self.ko, self.vo = part, ko, vo
        (self.s0, self.r0, self.acc, self.s1, self.r1, self.acc2, self.r2, self.res) = sc[:8]
        self.ss, self.rs, self.zs, self.zr = sc[8:]
        self.c, self.r, self.z, self.xy, self.role, self.mate = place()
        self.ylo = self.r // 2
        self.other_y = (1 - self.ylo) * 2 + self.role
        self.far = (1 - self.ylo) * 2 + 1 - self.role

    def peers(self):
        out = [(self.c, self.mate), (self.c, self.far)]
        for s in range(1, NZ):
            out.append((self.xy * NZ + lax.rem(self.z + s, NZ), self.r))
        for s in range(1, 16):
            out.append(self.target(s)[:2])
        return out

    def target(self, s):
        me = self.xy * 2 + self.ylo
        other = lax.rem(me + s, 16)
        return (other // 2) * NZ + self.z, lax.rem(other, 2) * 2 + self.role, other

    def core_copy(self, k):
        return remote(self.s0.at[k], self.r0.at[k], self.ss.at[k], self.rs.at[k], self.c, self.mate)

    def core_start(self, k, cols):
        self.s0[k] = self.part[1 - self.role, :, cols].astype(jnp.bfloat16)
        self.core_copy(k).start()

    def chip_start(self):
        for k in range(KVH):
            self.core_copy(k).wait_recv()
            cols = slice(k * D, (k + 1) * D)
            total = self.part[self.role, :, cols] + self.r0[k].astype(jnp.float32)
            self.acc[:, cols] = total
            self.s1[:, cols] = total.astype(jnp.bfloat16)
        self.copies = []
        for s in range(1, 16):
            ctx, resp, other = self.target(s)
            rows = self.s1.at[pl.ds(pl.multiple_of(other * 32, 32), 32)]
            self.copies.append(remote(rows, self.r1.at[s], self.ss.at[8 + s], self.rs.at[8 + s], ctx, resp))
        for copy in self.copies:
            copy.start()

    def z_copies(self):
        out = []
        for q in range(4):
            to = 4 * self.ylo + q
            copy = remote(
                self.acc2.at[q], self.r2.at[self.z], self.zs.at[q], self.zr.at[self.z], self.xy * NZ + to, self.r
            )
            out.append((to != self.z, copy))
        return out

    def z_start(self):
        me = self.xy * 2 + self.ylo
        total = self.acc[pl.ds(pl.multiple_of(me * 32, 32), 32), :]
        for s, copy in enumerate(self.copies, 1):
            copy.wait_recv()
            total = total + self.r1[s].astype(jnp.float32)
        self.acc2[...] = total.reshape(4, 8, 512)
        for condition, copy in self.z_copies():
            Gather.when(condition, copy.start)

    def out_copies(self):
        block = self.res.at[self.role]
        places = (self.mate, self.other_y, self.far)
        return [
            remote(block, block, self.zs.at[4 + i], self.rs.at[4 + self.role], self.c, resp)
            for i, resp in enumerate(places)
        ]

    def owners_start(self):
        z = self.z

        @pl.when(z // 4 == self.ylo)
        def _():
            self.r2[z] = self.acc2[lax.rem(z, 4)]
            for i in range(NZ):

                @pl.when(z != i)
                def _(i=i):
                    slot = self.r2.at[i]
                    remote(slot, slot, self.zs.at[0], self.zr.at[i], self.c, self.r).wait_recv()

            total = self.r2[0]
            for i in range(1, NZ):
                total = total + self.r2[i]
            self.res[self.role] = total
            for copy in self.out_copies():
                copy.start()

    def finish(self):
        owner = self.z // 4 == self.ylo
        for i in range(2):

            @pl.when(jnp.logical_not(owner & (self.role == i)))
            def _(i=i):
                block = self.res.at[i]
                remote(block, block, self.zs.at[0], self.rs.at[4 + i], self.c, self.mate).wait_recv()

        self.ko[...] = self.res[0].astype(jnp.bfloat16)
        self.vo[...] = self.res[1].astype(jnp.bfloat16)
        for copy in [self.core_copy(k) for k in range(KVH)] + self.copies:
            copy.wait_send()
        for condition, copy in self.z_copies():
            Gather.when(condition, copy.wait_send)

        @pl.when(owner)
        def _():
            for copy in self.out_copies():
                copy.wait_send()


REDUCE_SCRATCH = [
    pltpu.VMEM((KVH, PR, D), jnp.bfloat16),
    pltpu.VMEM((KVH, PR, D), jnp.bfloat16),
    pltpu.VMEM((PR, 512), jnp.float32),
    pltpu.VMEM((PR, 512), jnp.bfloat16),
    pltpu.VMEM((16, 32, 512), jnp.bfloat16),
    pltpu.VMEM((4, 8, 512), jnp.float32),
    pltpu.VMEM((NZ, 8, 512), jnp.float32),
    pltpu.VMEM((2, 8, 512), jnp.float32),
    pltpu.SemaphoreType.DMA((24,)),
    pltpu.SemaphoreType.DMA((24,)),
    pltpu.SemaphoreType.DMA((8,)),
    pltpu.SemaphoreType.DMA((8,)),
]


GATHER_SCRATCH = [
    pltpu.VMEM((2, 17, T, 512), jnp.bfloat16),
    pltpu.VMEM((2, PR, 512), jnp.bfloat16),
    pltpu.VMEM((NZ, 8, 512), jnp.float32),
    pltpu.SemaphoreType.DMA((6 * ROUNDS,)),
    pltpu.SemaphoreType.DMA((2 * OWN,)),
    pltpu.SemaphoreType.DMA((16,)),
    pltpu.SemaphoreType.DMA((16,)),
]
OWN_SCRATCH = [
    pltpu.VMEM((T, HQ * D), jnp.bfloat16),
    pltpu.VMEM((T, HQ * D), jnp.bfloat16),
    pltpu.VMEM((2, PR, 512), jnp.float32),
    pltpu.SemaphoreType.DMA((4,)),
]


def kernel(q_in, do_in, k_in, v_in, pk, pv, lengths, dq, ko, vo, *scratch):
    ng, no, na = len(GATHER_SCRATCH), len(OWN_SCRATCH), len(ATTEND_SCRATCH)
    gather_refs, own_refs = scratch[:ng], scratch[ng : ng + no]
    q, do, part, sems = own_refs
    g = Gather(*gather_refs)
    r = Reduce(part, ko, vo, scratch[ng + no + na :])
    a = Attend(q, do, g.kv, g.pg, lengths, scratch[ng + no : ng + no + na])
    loads = [
        pltpu.make_async_copy(k_in, g.kv.at[0, OWN], sems.at[0]),
        pltpu.make_async_copy(v_in, g.kv.at[1, OWN], sems.at[1]),
        pltpu.make_async_copy(q_in, q, sems.at[2]),
        pltpu.make_async_copy(do_in, do, sems.at[3]),
    ]
    for copy in loads:
        copy.start()
    barrier, arrivals = greet(r.peers())
    for copy in loads:
        copy.wait()
    a.prepare()
    pl.semaphore_wait(barrier, arrivals)
    g.prompt_z(pk, pv)
    words = g.tables()
    g.start_round(0, 0, words)
    g.start_round(1, 0, words)
    g.prompt_pair()
    a.slot_block(OWN)

    def one_round(t, words):
        later = g.following(words)
        for half in range(2):
            g.take_round(half, words)
            pl.when(t < ROUNDS)(lambda half=half: g.start_round(half, t, later))
        pl.when(t == 1)(lambda: g.prompt_hop(0))
        pl.when(t == 3)(lambda: g.prompt_hop(3))
        slots = g.received(words)

        @pl.loop(0, 3)
        def _(i):
            slot = jnp.where(i == 0, slots[0], jnp.where(i == 1, slots[1], slots[2]))
            pl.when(slot != NONE)(lambda: a.slot_block(slot))

        pl.when(t == 1)(lambda: g.prompt_hop(1))
        pl.when(t == 2)(lambda: g.prompt_hop(2))
        pl.when(t == 3)(g.prompt_done)
        low = 1 * (t > 3).astype(jnp.int32) + 2 * (t > 4).astype(jnp.int32) + 1 * (t > 5).astype(jnp.int32)
        high = 1 * (t >= 3).astype(jnp.int32) + 2 * (t >= 4).astype(jnp.int32) + 1 * (t >= 5).astype(jnp.int32)

        @pl.loop(0, 2)
        def _(i):
            pl.when(low + i < high)(lambda: a.prompt_block(low + i))

        return later

    lax.fori_loop(1, ROUNDS + 1, one_round, words)
    a.settle()
    a.prompt_grads(part, r.core_start)
    r.chip_start()
    a.prompt_dq()
    a.slot_grads(OWN)

    @pl.loop(0, 5)
    def _(pair):
        a.pair_grads(pair)

    r.z_start()

    @pl.loop(5, 8)
    def _(pair):
        a.pair_grads(pair)

    r.owners_start()
    a.store(dq)
    r.finish()
    g.prompt_sent()
    g.finish(words)


VM = pl.BlockSpec(memory_space=pltpu.VMEM)
SM = pl.BlockSpec(memory_space=pltpu.SMEM)
ANY = pl.BlockSpec(memory_space=pl.ANY)
MIB = 2**20


def body(queries, cotangent, sampled_keys, sampled_values, prompt_keys, prompt_values, lengths):
    dq, ko, vo = pl.pallas_call(
        kernel,
        out_shape=(
            jax.ShapeDtypeStruct((T, HQ * D), jnp.bfloat16),
            jax.ShapeDtypeStruct((8, 512), jnp.bfloat16),
            jax.ShapeDtypeStruct((8, 512), jnp.bfloat16),
        ),
        in_specs=[ANY] * 4 + [VM] * 2 + [SM],
        out_specs=(VM, VM, VM),
        scratch_shapes=GATHER_SCRATCH + OWN_SCRATCH + ATTEND_SCRATCH + REDUCE_SCRATCH,
        compiler_params=pltpu.CompilerParams(
            collective_id=0, has_side_effects=True, vmem_limit_bytes=62 * MIB
        ),
        name="shared_prompt_backward",
    )(queries[0], cotangent[0], sampled_keys[0], sampled_values[0], prompt_keys, prompt_values, lengths)
    return dq[None], ko, vo


def solution(mesh):
    rows = P("resp", "ctx", None)
    in_specs = (rows, rows, rows, rows, P("ctx", None), P("ctx", None), P("resp", None))
    out_specs = (rows, P("ctx", None), P("ctx", None))
    return jax.shard_map(body, mesh=mesh, in_specs=in_specs, out_specs=out_specs, check_vma=False)
```
